32 devices in a mesh: groups: 1, expert: 32 (over z, y, x, core).
Axes of the slice: x: 2, y: 2, z: 4, core: 2. Of those that a mesh axis runs over, the one named last changes fastest.
Arguments:
- tokens: bfloat16 [1024, 6144], P(('groups', 'expert')), may hold values from -6 to 6
- routes: int32 [4096, 2], P(('groups', 'expert')), may hold values from 0 to 7, all different within a row; in each aligned block of 128 rows (0 to 127, 128 to 255, ...) at most 48 rows name the same one
- gates: float32 [4096, 2], P(('groups', 'expert')), may hold values from 0.1 to 1
- w_up: bfloat16 [32, 1536, 512], P('expert'), may hold values from -0.15625 to 0.15625
- w_down: bfloat16 [32, 512, 1536], P('expert'), may hold values from -0.125 to 0.125
- cotangent: bfloat16 [1024, 6144], P(('groups', 'expert')), may hold values from -6 to 6
Outputs:
- mixed: bfloat16 [1024, 6144], P(('groups', 'expert'))
- d_tokens: bfloat16 [1024, 6144], P(('groups', 'expert'))
- d_up: float32 [32, 1536, 512], P(('groups', 'expert'))
- d_down: float32 [32, 512, 1536], P(('groups', 'expert'))
The draws below stay inside these ranges and needn't reach their ends.
Inputs may be any that keep to these rules, and one draw needn't show every extreme that they name: `routes`: the two experts of a row differ; in the rows of one device (aligned blocks of 128 rows) no expert is named more than 48 times, a bound that some block reaches.
All inputs are finite; a program needn't handle non-finite values.
Results may differ from the reference program's by a relative error of at most 0.0072.
Values may be sent and summed in bfloat16 or wider, within the bound.
No kernel may reach another device: no remote copies, remote signals or barrier semaphores. Data moves between devices by JAX's collectives and lax.ppermute only.
A program may use at most 128 MiB of HBM per device.

```python
import math
import jax
import jax.numpy as jnp
import numpy as np
from jax import lax

HEADS = 4
HD = 1536
D = 6144
FF = 2048
SPLIT = 4
EXPERTS = 8
TOK_DEV = 32
CAP = 48
TOKENS = 1024
SUBS = 4096
N_EXPERT = 32


def steps_of(key, dims, split, smallest, high):
    loudness, own = 1.0, jax.random.fold_in(key, 6)
    for dim, shards_of in split:
        heights = jnp.exp(jax.random.uniform(jax.random.fold_in(own, dim), (shards_of,), jnp.float32, smallest / len(split), high / len(split)))
        loudness = loudness * jnp.repeat(heights, dims[dim] // shards_of).reshape([-1 if axis == dim else 1 for axis in range(len(dims))])
    return loudness


def deal_out(key, own, number, rows, number_of, top, most, slope):
    order = jax.random.permutation(key, number_of)
    packed, usual = portions_of(number_of, rows * top, most, slope, True), portions_of(number_of, rows * top, most, slope, False)
    places = jnp.arange(number_of)

    def named(tallies, offset_by):
        used = int((tallies > 0).sum())
        fixed = max(1, used // 4)
        passed = fixed + (places - fixed + offset_by * (used - fixed)) % max(1, number_of - fixed)
        return jnp.zeros((number_of,), jnp.int32).at[order[jnp.where(places < fixed, places, passed)]].set(jnp.asarray(tallies, jnp.int32))

    tallies = jnp.where(number % 4 == 0, named(packed, number // 4), named(usual, number - number // 4 - 1))
    mixed = jax.random.permutation(jax.random.fold_in(own, 3), number_of)
    donor, sink = mixed[0:number_of // 2 * 2:2], mixed[1:number_of // 2 * 2:2]
    room = jnp.minimum(tallies[donor] - 1, most - tallies[sink]) // 2
    room = jnp.where((donor == order[0]) | (sink == order[0]) | (tallies[sink] == 0), 0, jnp.maximum(room, 0))
    passed = jax.random.randint(jax.random.fold_in(own, 4), (number_of // 2,), 0, 1 << 20) % (room + 1)
    tallies = tallies.at[donor].add(-passed).at[sink].add(passed)
    members = jnp.searchsorted(jnp.cumsum(tallies), jnp.arange(rows * top), side="right").astype(jnp.int32)
    table = members.reshape(top, rows).T
    table = table[jax.random.permutation(jax.random.fold_in(own, 1), rows)]
    offset_by = jax.random.randint(jax.random.fold_in(own, 2), (rows, 1), 0, top)
    return jnp.take_along_axis(table, (jnp.arange(top)[None, :] + offset_by) % top, axis=1)


def portions_of(number_of, total, bound, lean, full):
    loads = [(1 << 20) // math.isqrt(rank ** lean) + 1 for rank in range(1, number_of + 1)]
    largest = bound if full else min(bound, max(-(-total // number_of), total * loads[0] // sum(loads)))
    least = 1 if total - largest >= number_of - 1 else 0
    given, surplus = [largest] + [least] * (number_of - 1), total - largest - least * (number_of - 1)
    while surplus > 0:
        candidates = [i for i in range(1, number_of) if given[i] < largest] or [i for i in range(1, number_of) if given[i] < bound]
        whole, left = sum([loads[i] for i in candidates]), surplus
        for i in candidates:
            more = min(bound - given[i], max(1, left * loads[i] // whole), surplus)
            given[i] = given[i] + more
            surplus = surplus - more
    return np.array(given)


def noise(stream_key, dims, deviation, reach, shards=(), held_as=jnp.bfloat16):
    gain = steps_of(stream_key, dims, shards, -0.22, 0.18) if shards else 1.0
    entries = jax.random.normal(stream_key, dims, jnp.float32) * deviation * gain
    return jnp.minimum(jnp.maximum(entries, -reach), reach).astype(held_as)


def setup_inputs(seed: int = 0, part: int = 0) -> dict:
    key_of = jax.random.split(jax.random.key(seed), 7)
    own_keys = jax.random.split(jax.random.fold_in(key_of[6], part), 7)
    tokens = noise(own_keys[0], (TOKENS, D), 1.0, 6.0, ((0, 32),))
    routes_keys = jax.random.split(jax.random.fold_in(own_keys[1], 1), SUBS // (HEADS * TOK_DEV))
    routes_turns = jax.random.permutation(jax.random.fold_in(own_keys[1], 3), SUBS // (HEADS * TOK_DEV))
    routes = jax.vmap(lambda own, number: deal_out(jax.random.fold_in(own_keys[1], 2), own, number, HEADS * TOK_DEV, EXPERTS, 2, CAP, 2))(routes_keys, routes_turns).reshape((SUBS, 2))
    gates = jnp.clip(0.1 + 0.9 * jax.random.uniform(own_keys[2], (SUBS, 2), jnp.float32) ** steps_of(own_keys[2], (SUBS, 2), ((0, 32),), -0.2, 0.2), 0.1, 1.0)
    w_up = noise(key_of[3], (EXPERTS * SPLIT, HD, FF // SPLIT), HD ** -0.5, 0.15625, ((0, 32),))
    w_down = noise(key_of[4], (EXPERTS * SPLIT, FF // SPLIT, HD), FF ** -0.5, 0.125, ((0, 32),))
    cotangent = noise(own_keys[5], (TOKENS, D), 1.0, 6.0, ((0, 32),))
    return {"tokens": tokens, "routes": routes, "gates": gates, "w_up": w_up, "w_down": w_down, "cotangent": cotangent}


def silu_grad(values):
    gate_sig = jax.nn.sigmoid(values)
    return gate_sig * (1.0 + values * (1.0 - gate_sig))

def reference(tokens, routes, gates, w_up, w_down, cotangent):
    block_hidden = FF // SPLIT
    sub_rows = tokens.reshape(SUBS, HD)
    grad_rows = cotangent.reshape(SUBS, HD)
    per_device = routes.reshape(N_EXPERT, 2 * HEADS * TOK_DEV)
    onehot = (per_device[:, :, None] == jnp.arange(EXPERTS, dtype=jnp.int32)[None, None, :]).astype(jnp.int32)
    slot_rank = jnp.cumsum(onehot, axis=1) - 1
    slot_of = lax.optimization_barrier(jnp.sum(slot_rank * onehot, axis=2))
    device_ids = jnp.arange(N_EXPERT, dtype=jnp.int32)[:, None]
    target = ((device_ids * EXPERTS + per_device) * CAP + slot_of).astype(jnp.int32)
    flat_target = target.reshape(-1)
    pair_targets = target.reshape(SUBS, 2)
    slot_total = N_EXPERT * EXPERTS * CAP
    doubled = jnp.repeat(sub_rows, 2, axis=0)
    inputs = jnp.zeros((slot_total, HD), jnp.bfloat16).at[flat_target].set(doubled)
    scaled = (gates.reshape(-1, 1) * jnp.repeat(grad_rows, 2, axis=0).astype(jnp.float32)).astype(jnp.bfloat16)
    grads_in = jnp.zeros((slot_total, HD), jnp.bfloat16).at[flat_target].set(scaled)

    def by_expert(buffer):
        return buffer.reshape(N_EXPERT, EXPERTS, CAP, HD).transpose(1, 0, 2, 3).reshape(EXPERTS, N_EXPERT * CAP, HD)

    def to_devices(buffer):
        return buffer.reshape(EXPERTS, N_EXPERT, CAP, HD).transpose(1, 0, 2, 3).reshape(slot_total, HD)
    up_full = w_up.reshape(EXPERTS, SPLIT, HD, block_hidden)
    down_full = w_down.reshape(EXPERTS, SPLIT, block_hidden, HD)

    def one_expert(operands):
        rows_in, grad_out, up_blocks, down_blocks = operands
        up_matrix = up_blocks.transpose(1, 0, 2).reshape(HD, FF)
        down_matrix = down_blocks.reshape(FF, HD)
        pre_act = jnp.dot(rows_in, up_matrix, preferred_element_type=jnp.float32)
        hidden = jax.nn.silu(pre_act).astype(jnp.bfloat16)
        block_out = jnp.einsum('rsf,sfh->srh', hidden.reshape(-1, SPLIT, block_hidden).astype(jnp.float32), down_blocks.astype(jnp.float32), precision=lax.Precision.HIGHEST).astype(jnp.bfloat16)
        block_out = lax.optimization_barrier(block_out)
        expert_out = lax.optimization_barrier(jnp.sum(block_out.astype(jnp.float32), axis=0)).astype(jnp.bfloat16)
        grad_hidden = jnp.dot(grad_out, down_matrix.T, preferred_element_type=jnp.float32)
        grad_pre = (grad_hidden * silu_grad(pre_act)).astype(jnp.bfloat16)
        grad_down = jnp.dot(hidden.T, grad_out, preferred_element_type=jnp.float32)
        grad_up = jnp.dot(rows_in.T, grad_pre, preferred_element_type=jnp.float32)
        block_back = jnp.einsum('rsf,shf->srh', grad_pre.reshape(-1, SPLIT, block_hidden).astype(jnp.float32), up_blocks.astype(jnp.float32), precision=lax.Precision.HIGHEST).astype(jnp.bfloat16)
        block_back = lax.optimization_barrier(block_back)
        back_out = lax.optimization_barrier(jnp.sum(block_back.astype(jnp.float32), axis=0)).astype(jnp.bfloat16)
        return (expert_out, back_out, grad_up, grad_down)
    expert_out, back_out, grad_up, grad_down = lax.map(one_expert, (by_expert(inputs), by_expert(grads_in), up_full, down_full))
    out_flat = to_devices(expert_out)
    back_flat = to_devices(back_out)
    picked = out_flat[pair_targets].astype(jnp.float32)
    mixed = lax.optimization_barrier(jnp.sum(gates[:, :, None] * picked, axis=1)).astype(jnp.bfloat16).reshape(TOKENS, D)
    token_grad = lax.optimization_barrier(jnp.sum(back_flat[pair_targets].astype(jnp.float32), axis=1)).astype(jnp.bfloat16).reshape(TOKENS, D)
    d_up = grad_up.reshape(EXPERTS, HD, SPLIT, block_hidden).transpose(0, 2, 1, 3).reshape(EXPERTS * SPLIT, HD, block_hidden)
    d_down = grad_down.reshape(EXPERTS * SPLIT, block_hidden, HD)
    return (mixed, token_grad, d_up, d_down)
```

```python
import functools
import jax
import jax.numpy as jnp
from jax import lax
from jax.experimental import pallas as pl
from jax.experimental.pallas import tpu as pltpu
from jax.sharding import PartitionSpec as P

HEADS = 4
SPLIT = 4
VMEM = 48 * 1024 * 1024


def swap(value, bits):
    count = lax.axis_size("expert")
    return lax.ppermute(value, "expert", [(i, i ^ bits) for i in range(count)])


def silu_grad(values):
    gate_sig = jax.nn.sigmoid(values)
    return gate_sig * (1.0 + values * (1.0 - gate_sig))


def heads_of(index, per_head):
    head = jnp.zeros_like(index)
    for h in range(1, HEADS):
        head = head + (index >= h * per_head).astype(jnp.int32)
    return head


def natural(index, per_head):
    head = heads_of(index, per_head)
    return HEADS * (index - per_head * head) + head


def iota(shape, dim):
    return lax.broadcasted_iota(jnp.int32, shape, dim)


def by_head(pair_rows):
    rows = pair_rows.shape[1]
    place = natural(iota((rows, rows), 1), rows // HEADS)
    turn = (iota((rows, rows), 0) == place).astype(jnp.float32)
    return jnp.dot(
        pair_rows, turn, preferred_element_type=jnp.float32, precision=lax.Precision.HIGHEST
    )


def positions(me_ref, routes_ref, experts_all, capacity):
    rows = routes_ref.shape[1]
    routes = by_head(routes_ref[...].astype(jnp.float32)).astype(jnp.int32)
    first, second = routes[0:1], routes[1:2]
    expert = iota((experts_all, rows), 0)
    named = ((expert == first) | (expert == second)).astype(jnp.bfloat16)
    earlier = (
        natural(iota((rows, rows), 0), rows // HEADS)
        < natural(iota((rows, rows), 1), rows // HEADS)
    ).astype(jnp.bfloat16)
    rank = jnp.dot(named, earlier, preferred_element_type=jnp.float32).astype(jnp.int32)
    where_to = (expert ^ me_ref[0]) * capacity + rank
    return tuple(
        jnp.sum(jnp.where(expert == which, where_to, 0), axis=0, keepdims=True)
        for which in (first, second)
    )


def stacked(tokens_ref):
    feature = tokens_ref.shape[1] // HEADS
    return jnp.concatenate(
        [tokens_ref[:, h * feature : (h + 1) * feature] for h in range(HEADS)], axis=0
    )


def place_kernel(experts_all, capacity, gated, me_ref, routes_ref, gates_ref, tokens_ref, *blocks):
    rows = routes_ref.shape[1]
    first, second = positions(me_ref, routes_ref, experts_all, capacity)
    slot = iota((experts_all * capacity, rows), 0)
    at_first, at_second = slot == first, slot == second
    pick = (at_first | at_second).astype(jnp.bfloat16)
    placed = jnp.dot(pick, stacked(tokens_ref), preferred_element_type=jnp.float32)
    if gated:
        gates = by_head(gates_ref[...])
        weight = jnp.sum(
            jnp.where(at_first, gates[0:1], 0.0) + jnp.where(at_second, gates[1:2], 0.0),
            axis=1,
            keepdims=True,
        )
        placed = weight * placed
    placed = placed.astype(jnp.bfloat16)
    for m, block in enumerate(blocks):
        block[...] = placed[m * capacity : (m + 1) * capacity]


def column(row):
    count = row.shape[1]
    return jnp.sum(
        jnp.where(iota((count, count), 0) == iota((count, count), 1), row, jnp.zeros((), row.dtype)),
        axis=1,
        keepdims=True,
    )


def collect_kernel(experts_all, capacity, gated, me_ref, routes_ref, gates_ref, *refs):
    blocks, out_ref = refs[:-1], refs[-1]
    rows = routes_ref.shape[1]
    feature = out_ref.shape[1] // HEADS
    first, second = (column(t) for t in positions(me_ref, routes_ref, experts_all, capacity))
    values = jnp.concatenate([block[...] for block in blocks], axis=0)
    slot = iota((rows, experts_all * capacity), 1)
    at_first, at_second = slot == first, slot == second
    if gated:
        gates = by_head(gates_ref[...])
        total = column(gates[0:1]) * jnp.dot(
            at_first.astype(jnp.bfloat16), values, preferred_element_type=jnp.float32
        ) + column(gates[1:2]) * jnp.dot(
            at_second.astype(jnp.bfloat16), values, preferred_element_type=jnp.float32
        )
    else:
        total = jnp.dot(
            (at_first | at_second).astype(jnp.bfloat16), values, preferred_element_type=jnp.float32
        )
    total = total.astype(jnp.bfloat16)
    per_head = rows // HEADS
    for h in range(HEADS):
        out_ref[:, h * feature : (h + 1) * feature] = total[h * per_head : (h + 1) * per_head]


def place(me, routes, gates, tokens, experts_all, capacity, gated):
    feature = tokens.shape[1] // HEADS
    vmem = pl.BlockSpec(memory_space=pltpu.VMEM)
    block = jax.ShapeDtypeStruct((capacity, feature), jnp.bfloat16)
    return pl.pallas_call(
        functools.partial(place_kernel, experts_all, capacity, gated),
        out_shape=[block] * experts_all,
        in_specs=[pl.BlockSpec(memory_space=pltpu.SMEM), vmem, vmem, vmem],
        out_specs=[vmem] * experts_all,
        compiler_params=pltpu.CompilerParams(vmem_limit_bytes=VMEM),
    )(me, routes, gates, tokens)


def collect(me, routes, gates, blocks, tok_local, experts_all, capacity, gated):
    feature = blocks[0].shape[1]
    vmem = pl.BlockSpec(memory_space=pltpu.VMEM)
    return pl.pallas_call(
        functools.partial(collect_kernel, experts_all, capacity, gated),
        out_shape=jax.ShapeDtypeStruct((tok_local, HEADS * feature), jnp.bfloat16),
        in_specs=[pl.BlockSpec(memory_space=pltpu.SMEM)] + [vmem] * (2 + experts_all),
        out_specs=vmem,
        compiler_params=pltpu.CompilerParams(vmem_limit_bytes=VMEM),
    )(me, routes, gates, *blocks)


def spread(blocks, groups):
    sent = []
    for group in groups:
        mine = jnp.concatenate([swap(blocks[m], SPLIT * m) if m else blocks[m] for m in group])
        sent.append((mine, swap(mine, 2)))
    return [jnp.concatenate(pair) for pair in sent]


def bring_back(partials, groups, capacity):
    back = {}
    for group, partial in zip(groups, partials):
        half = len(group) * capacity
        total = (
            partial[:half].astype(jnp.float32) + swap(partial[half:], 2).astype(jnp.float32)
        ).astype(jnp.bfloat16)
        for i, m in enumerate(group):
            block = total[i * capacity : (i + 1) * capacity]
            back[m] = swap(block, SPLIT * m) if m else block
    return [back[m] for m in sorted(back)]


def dot(a, b, dims):
    return lax.dot_general(a, b, (dims, ((), ())), preferred_element_type=jnp.float32)


def on_device(tokens, routes, gates, w_up, w_down, cotangent):
    devices = lax.axis_size("expert")
    experts_all = devices // SPLIT
    tok_local = tokens.shape[0]
    capacity = SPLIT * (
        (6 * HEADS * tok_local + 2 * experts_all * SPLIT - 1) // (2 * experts_all * SPLIT)
    )
    capacity = 16 * ((capacity + 15) // 16)
    me = (lax.axis_index("expert") // SPLIT).astype(jnp.int32).reshape(1)
    routes, gates = routes.T, gates.T
    groups = [list(range(0, experts_all, 2)), list(range(1, experts_all, 2))]

    x_blocks = place(me, routes, gates, tokens, experts_all, capacity, False)
    g_blocks = place(me, routes, gates, cotangent, experts_all, capacity, True)
    up_own, down_own = w_up[0], w_down[0]
    block_hidden = up_own.shape[1]
    up = jnp.concatenate([up_own, swap(up_own, 1)], axis=1)
    down = jnp.concatenate([down_own, swap(down_own, 1)], axis=0)

    rows_in = spread(x_blocks, groups)
    pre_act = [dot(rows, up, ((1,), (0,))) for rows in rows_in]
    hidden = [jax.nn.silu(pre).astype(jnp.bfloat16) for pre in pre_act]
    partial = [dot(hid, down, ((1,), (0,))).astype(jnp.bfloat16) for hid in hidden]
    outs = bring_back(partial, groups, capacity)
    mixed = collect(me, routes, gates, outs, tok_local, experts_all, capacity, True)

    grads_in = spread(g_blocks, groups)
    grad_pre = [
        (dot(grad, down, ((1,), (1,))) * silu_grad(pre)).astype(jnp.bfloat16)
        for grad, pre in zip(grads_in, pre_act)
    ]
    back = [dot(grad, up, ((1,), (1,))).astype(jnp.bfloat16) for grad in grad_pre]
    backs = bring_back(back, groups, capacity)
    token_grad = collect(me, routes, gates, backs, tok_local, experts_all, capacity, False)

    x_all, g_all = jnp.concatenate(rows_in), jnp.concatenate(grads_in)
    hid_all, pre_all = jnp.concatenate(hidden), jnp.concatenate(grad_pre)
    x_other, g_other = swap(x_all, 1), swap(g_all, 1)
    hid_other = swap(hid_all[:, block_hidden:], 1)
    pre_other = swap(pre_all[:, block_hidden:], 1)
    grad_down = dot(hid_all[:, :block_hidden], g_all, ((0,), (0,))) + dot(
        hid_other, g_other, ((0,), (0,))
    )
    grad_up = dot(x_all, pre_all[:, :block_hidden], ((0,), (0,))) + dot(
        x_other, pre_other, ((0,), (0,))
    )
    return (mixed, token_grad, grad_up[None], grad_down[None])


def solution(mesh):
    placed = (
        P(("groups", "expert"), None),
        P(("groups", "expert"), None),
        P(("groups", "expert"), None),
        P("expert", None, None),
        P("expert", None, None),
        P(("groups", "expert"), None),
    )
    return jax.shard_map(
        on_device,
        mesh=mesh,
        in_specs=placed,
        out_specs=(
            P(("groups", "expert"), None),
            P(("groups", "expert"), None),
            P(("groups", "expert"), None, None),
            P(("groups", "expert"), None, None),
        ),
        check_vma=False,
    )
```

```python
import functools
import jax
import jax.numpy as jnp
from jax import lax
from jax.experimental import pallas as pl
from jax.experimental.pallas import tpu as pltpu
from jax.sharding import PartitionSpec as P

HEADS = 4
SPLIT = 4
VMEM = 20 * 1024 * 1024
FREE = pl.CostEstimate(flops=1, bytes_accessed=1, transcendentals=0)


def swap(value, bits, odd_bits=0):
    count = lax.axis_size("expert")
    return lax.ppermute(
        value, "expert", [(i, i ^ bits ^ (odd_bits if i % 2 else 0)) for i in range(count)]
    )


class Order:
    def __init__(self):
        self.last = ()

    def wait(self, *values):
        values = lax.optimization_barrier((*values, *self.last))[: len(values)]
        self.last = values[:1]
        return values[0] if len(values) == 1 else values

    def done(self, value):
        self.last = (value,)

    def begin(self, send, value, *where):
        return send(lax.optimization_barrier((value, *self.last))[0], *where)


def silu_grad(values):
    gate_sig = jax.nn.sigmoid(values)
    return gate_sig * (1.0 + values * (1.0 - gate_sig))


def heads_of(index, per_head):
    head = jnp.zeros_like(index)
    for h in range(1, HEADS):
        head = head + (index >= h * per_head).astype(jnp.int32)
    return head


def natural(index, per_head):
    head = heads_of(index, per_head)
    return HEADS * (index - per_head * head) + head


def iota(shape, dim):
    return lax.broadcasted_iota(jnp.int32, shape, dim)


def by_head(pair_rows):
    rows = pair_rows.shape[1]
    place = natural(iota((rows, rows), 1), rows // HEADS)
    turn = (iota((rows, rows), 0) == place).astype(jnp.float32)
    return jnp.dot(
        pair_rows, turn, preferred_element_type=jnp.float32, precision=lax.Precision.HIGHEST
    )


def ranks(me, routes_ref, experts_all):
    rows = routes_ref.shape[1]
    routes = by_head(routes_ref[...].astype(jnp.float32)).astype(jnp.int32)
    first, second = routes[0:1], routes[1:2]
    expert = iota((experts_all, rows), 0)
    named = ((expert == first) | (expert == second)).astype(jnp.bfloat16)
    earlier = (
        natural(iota((rows, rows), 0), rows // HEADS)
        < natural(iota((rows, rows), 1), rows // HEADS)
    ).astype(jnp.bfloat16)
    rank = jnp.dot(named, earlier, preferred_element_type=jnp.float32).astype(jnp.int32)
    return [
        (which ^ me, jnp.sum(jnp.where(expert == which, rank, 0), axis=0, keepdims=True))
        for which in (first, second)
    ]


def stacked(tokens_ref):
    feature = tokens_ref.shape[1] // HEADS
    return jnp.concatenate(
        [tokens_ref[:, h * feature : (h + 1) * feature] for h in range(HEADS)], axis=0
    )


def place_kernel(experts_all, capacity, gated, index_ref, *refs):
    routes_refs, refs = refs[:2], refs[2:]
    if gated:
        gates_refs, refs = refs[:2], refs[2:]
    tokens_refs, blocks = refs[:2], refs[2:]
    rows = routes_refs[0].shape[1]
    me, core = index_ref[0] // SPLIT, index_ref[0] % 2
    slot = iota((experts_all * capacity, rows), 0)
    picks, weight = [], 0.0
    for source in range(2):
        hits = []
        for distance, rank in ranks(me, routes_refs[source], experts_all):
            spot = ((distance >> 1) * 2 + source) * capacity + rank
            hits.append(slot == jnp.where((distance & 1) == core, spot, -1))
        picks.append((hits[0] | hits[1]).astype(jnp.bfloat16))
        if gated:
            gates = by_head(gates_refs[source][...])
            for k in range(2):
                weight = weight + jnp.where(hits[k], gates[k : k + 1], 0.0)
    placed = jnp.dot(
        jnp.concatenate(picks, axis=1),
        jnp.concatenate([stacked(ref) for ref in tokens_refs], axis=0),
        preferred_element_type=jnp.float32,
    )
    if gated:
        placed = jnp.sum(weight, axis=1, keepdims=True) * placed
    placed = placed.astype(jnp.bfloat16)
    for m, block in enumerate(blocks):
        block[...] = placed[2 * m * capacity : 2 * (m + 1) * capacity]


def column(row):
    count = row.shape[1]
    return jnp.sum(
        jnp.where(iota((count, count), 0) == iota((count, count), 1), row, jnp.zeros((), row.dtype)),
        axis=1,
        keepdims=True,
    )


def collect_kernel(experts_all, capacity, gated, index_ref, routes_ref, *refs):
    if gated:
        gates_ref, refs = refs[0], refs[1:]
    blocks, other_ref, out_ref = refs[:-2], refs[-2], refs[-1]
    rows = routes_ref.shape[1]
    feature = out_ref.shape[1] // HEADS
    me, core = index_ref[0] // SPLIT, index_ref[0] % 2
    values = jnp.concatenate([block[:capacity] for block in blocks] + [other_ref[...]], axis=0)
    slot = iota((rows, experts_all * capacity), 1)
    hits = []
    for distance, rank in ranks(me, routes_ref, experts_all):
        far = ((distance & 1) != core).astype(jnp.int32)
        spot = (far * (experts_all // 2) + (distance >> 1)) * capacity + rank
        hits.append(slot == column(spot))
    if gated:
        gates = by_head(gates_ref[...])
        total = sum(
            column(gates[k : k + 1])
            * jnp.dot(
                hits[k].astype(jnp.bfloat16), values, preferred_element_type=jnp.float32
            )
            for k in range(2)
        )
    else:
        total = jnp.dot(
            (hits[0] | hits[1]).astype(jnp.bfloat16), values, preferred_element_type=jnp.float32
        )
    total = total.astype(jnp.bfloat16)
    per_head = rows // HEADS
    for h in range(HEADS):
        out_ref[:, h * feature : (h + 1) * feature] = total[h * per_head : (h + 1) * per_head]


def place(index, routes, gates, tokens, experts_all, capacity):
    feature = tokens[0].shape[1] // HEADS
    operands = [*routes, *gates, *tokens]
    block = jax.ShapeDtypeStruct((2 * capacity, feature), jnp.bfloat16)
    return pl.pallas_call(
        functools.partial(place_kernel, experts_all, capacity, bool(gates)),
        out_shape=[block] * (experts_all // 2),
        in_specs=[pl.BlockSpec(memory_space=pltpu.SMEM)] + [pl.BlockSpec()] * len(operands),
        out_specs=[pl.BlockSpec(memory_space=pltpu.VMEM)] * (experts_all // 2),
        cost_estimate=FREE,
        compiler_params=pltpu.CompilerParams(vmem_limit_bytes=VMEM),
    )(index, *operands)


def collect(index, routes, gates, blocks, other, tok_local, experts_all, capacity):
    feature = other.shape[1]
    vmem = pl.BlockSpec(memory_space=pltpu.VMEM)
    operands = [routes, *gates, *blocks, other]
    return pl.pallas_call(
        functools.partial(collect_kernel, experts_all, capacity, bool(gates)),
        out_shape=jax.ShapeDtypeStruct((tok_local, HEADS * feature), jnp.bfloat16),
        in_specs=[pl.BlockSpec(memory_space=pltpu.SMEM)] + [vmem] * len(operands),
        out_specs=vmem,
        cost_estimate=FREE,
        compiler_params=pltpu.CompilerParams(vmem_limit_bytes=VMEM),
    )(index, *operands)


def dot(a, b, dims):
    return lax.dot_general(a, b, (dims, ((), ())), preferred_element_type=jnp.float32)


def call(kernel, out_shape, *operands):
    vmem = pl.BlockSpec(memory_space=pltpu.VMEM)
    return pl.pallas_call(
        kernel,
        out_shape=[jax.ShapeDtypeStruct(shape, dtype) for shape, dtype in out_shape],
        in_specs=[vmem] * len(operands),
        out_specs=[vmem] * len(out_shape),
        cost_estimate=FREE,
        compiler_params=pltpu.CompilerParams(vmem_limit_bytes=VMEM),
    )(*operands)


def forward_kernel(mine, far, up0, up1, down0, down1, pre0, pre1, hid0, hid1, part, part_far):
    rows = jnp.concatenate([mine[...], far[...]], axis=0)
    total = 0.0
    for up, down, pre, hid in ((up0, down0, pre0, hid0), (up1, down1, pre1, hid1)):
        act = dot(rows, up[...], ((1,), (0,)))
        pre[...] = act
        hidden = (act * jax.nn.sigmoid(act)).astype(jnp.bfloat16)
        hid[...] = hidden
        total = total + dot(hidden, down[...], ((1,), (0,)))
    total = total.astype(jnp.bfloat16)
    part[...] = total[: mine.shape[0]]
    part_far[...] = total[mine.shape[0] :]


def forward(mine, far, weights):
    rows, feature = mine.shape
    block = weights[0].shape[1]
    both = (2 * rows, block)
    pre0, pre1, hid0, hid1, part, part_far = call(
        forward_kernel,
        [(both, jnp.float32)] * 2 + [(both, jnp.bfloat16)] * 2 + [(mine.shape, jnp.bfloat16)] * 2,
        mine,
        far,
        *weights,
    )
    return (pre0, pre1), (hid0, hid1), part, part_far


def backward_kernel(mine, far, pre0, pre1, up0, up1, down0, down1, dpre0, dpre1, back, back_far):
    rows = jnp.concatenate([mine[...], far[...]], axis=0)
    total = 0.0
    for up, down, pre, dpre in ((up0, down0, pre0, dpre0), (up1, down1, pre1, dpre1)):
        grad = (dot(rows, down[...], ((1,), (1,))) * silu_grad(pre[...])).astype(jnp.bfloat16)
        dpre[...] = grad
        total = total + dot(grad, up[...], ((1,), (1,)))
    total = total.astype(jnp.bfloat16)
    back[...] = total[: mine.shape[0]]
    back_far[...] = total[mine.shape[0] :]


def backward(mine, far, pre, weights):
    dpre0, dpre1, back, back_far = call(
        backward_kernel,
        [(pre[0].shape, jnp.bfloat16)] * 2 + [(mine.shape, jnp.bfloat16)] * 2,
        mine,
        far,
        *pre,
        *weights,
    )
    return (dpre0, dpre1), back, back_far


def add_kernel(mine, far, *outs):
    total = (mine[...].astype(jnp.float32) + far[...].astype(jnp.float32)).astype(jnp.bfloat16)
    rows = outs[0].shape[0]
    for i, out in enumerate(outs):
        out[...] = total[i * rows : (i + 1) * rows]


def added(mine, far, group):
    shape = (mine.shape[0] // len(group), mine.shape[1])
    return dict(zip(group, call(add_kernel, [(shape, jnp.bfloat16)] * len(group), mine, far)))


def weight_kernel(lefts, rights, *refs):
    out, both = refs[-1], lefts + rights
    left = jnp.concatenate([ref[...] for ref in refs[:lefts]], axis=0)
    right = jnp.concatenate([ref[...] for ref in refs[lefts:both]], axis=0)
    total = dot(left, right, ((0,), (0,)))
    out[...] = total if len(refs) == both + 1 else total + refs[both][...]


def weight_grad(left, right, *other):
    shape = (left[0].shape[1], right[0].shape[1])
    return call(
        functools.partial(weight_kernel, len(left), len(right)), [(shape, jnp.float32)], *left, *right, *other
    )[0]


def hop(value, line):
    return swap(value, 2 * SPLIT * line, SPLIT)


def on_device(tokens, routes, gates, w_up, w_down, cotangent):
    devices = lax.axis_size("expert")
    experts_all = devices // SPLIT
    tok_local = tokens.shape[0]
    capacity = SPLIT * (
        (6 * HEADS * tok_local + 2 * experts_all * SPLIT - 1) // (2 * experts_all * SPLIT)
    )
    capacity = 16 * ((capacity + 15) // 16)
    index = lax.axis_index("expert").astype(jnp.int32).reshape(1)
    lines = experts_all // 2
    cuts = [0, lines // 2, lines - lines // 4, lines]
    near, mid, far = (list(range(a, b)) for a, b in zip(cuts, cuts[1:]))

    def joined(blocks, group):
        return blocks[group[0]] if len(group) == 1 else jnp.concatenate([blocks[m] for m in group])

    order = Order()

    def hops(blocks, group):
        return {m: order.begin(hop, blocks[m], m) for m in group}

    def come(sent):
        return dict(zip(sent, jax.tree.leaves(order.wait(*sent.values()))))

    def across(value):
        return order.begin(swap, value, 2)

    def core(value):
        return order.begin(swap, value, 1)

    def halves(blocks):
        return jnp.concatenate([blocks[m][capacity:] for m in sorted(blocks)])

    def ordered(blocks):
        return [blocks[m] for m in sorted(blocks)]

    sizes = (tok_local, experts_all, capacity)
    up_own, down_own = w_up[0], w_down[0]
    routes, gates = routes.T, gates.T

    tokens_other, routes_other = order.wait(core(tokens), core(routes))
    routes_both = (routes, routes_other)
    x_blocks = place(index, routes_both, (), (tokens, tokens_other), experts_all, capacity)
    order.done(x_blocks[0])
    x_near, x_mid, x_far, up_other = (
        hops(x_blocks, near), hops(x_blocks, mid), hops(x_blocks, far), core(up_own)
    )
    x0 = joined(come(x_near), near)
    x0_far, down_other = across(x0), core(down_own)
    up_other, down_other = order.wait(up_other, down_other)
    weights = (up_own, up_other, down_own, down_other)
    cotangent_other, gates_other = order.wait(core(cotangent), core(gates))
    g_blocks = place(
        index,
        routes_both,
        (gates, gates_other),
        (cotangent, cotangent_other),
        experts_all,
        capacity,
    )
    order.done(g_blocks[0])
    x1 = joined(come(x_mid), mid)
    x1_far, g_far = across(x1), hops(g_blocks, far)
    pre0, hid0, part0, part0_far = forward(x0, order.wait(x0_far), weights)
    order.done(part0_far)
    m0_far = across(part0_far)
    x2 = joined(come(x_far), far)
    x2_far, g_mid = across(x2), hops(g_blocks, mid)
    pre1, hid1, part1, part1_far = forward(x1, order.wait(x1_far), weights)
    order.done(part1_far)
    m1_far = across(part1_far)
    pre2, hid2, part2, part2_far = forward(x2, order.wait(x2_far), weights)
    order.done(part2_far)
    m2_far = across(part2_far)

    g2 = joined(come(g_far), far)
    g_near = hops(g_blocks, near[1:])
    m_sum = added(part0, order.wait(m0_far), near)
    order.done(m_sum[near[0]])
    g2_far = across(g2)
    g1 = joined(come(g_mid), mid)
    g_near |= hops(g_blocks, near[:1])
    g0 = joined(come(g_near), near)
    m_near = hops(m_sum, near)
    m_sum |= added(part1, order.wait(m1_far), mid)
    order.done(m_sum[mid[0]])
    g1_far = across(g1)
    m_home = come(m_near)
    m_mid = hops(m_sum, mid)
    m_sum |= added(part2, order.wait(m2_far), far)
    order.done(m_sum[far[0]])
    m_far, g0_far = hops(m_sum, far), across(g0)
    g2_far = order.wait(g2_far)
    dpre2, back2, back2_far = backward(g2, g2_far, pre2, weights)
    order.done(back2_far)
    b2_far = across(back2_far)
    g1_far = order.wait(g1_far)
    dpre1, back1, back1_far = backward(g1, g1_far, pre1, weights)
    order.done(back1_far)
    b1_far = across(back1_far)
    m_home |= come(m_mid)
    m_home |= come(m_far)
    m_other = core(halves(m_home))

    b_sum = added(back2, order.wait(b2_far), far)
    order.done(b_sum[far[0]])
    b_far = hops(b_sum, far)
    g0_far = order.wait(g0_far)
    dpre0, back0, back0_far = backward(g0, g0_far, pre0, weights)
    order.done(back0_far)
    b0_far = across(back0_far)
    mixed = collect(index, routes, (gates,), ordered(m_home), order.wait(m_other), *sizes)
    order.done(mixed)

    x_all = (x0, x0_far, x1, x1_far, x2, x2_far)
    g_all = (g0, g0_far, g1, g1_far, g2, g2_far)
    hid, dpre = zip(hid0, hid1, hid2), zip(dpre0, dpre1, dpre2)
    (hid_own, hid_other), (dpre_own, dpre_other) = hid, dpre
    down_part = weight_grad(hid_other, g_all)
    order.done(down_part)
    down_sent = core(down_part)
    up_part = weight_grad(x_all, dpre_other)
    order.done(up_part)
    up_sent = core(up_part)
    b_sum |= added(back1, order.wait(b1_far), mid)
    order.done(b_sum[mid[0]])
    b_mid = hops(b_sum, mid)
    grad_down = weight_grad(hid_own, g_all, order.wait(down_sent))
    order.done(grad_down)
    grad_up = weight_grad(x_all, dpre_own, order.wait(up_sent))
    order.done(grad_up)
    b_sum |= added(back0, order.wait(b0_far), near)
    order.done(b_sum[near[0]])
    b_home = come(b_far | b_mid | hops(b_sum, near))
    b_other = order.wait(core(halves(b_home)))
    token_grad = collect(index, routes, (), ordered(b_home), b_other, *sizes)
    return (mixed, token_grad, grad_up[None], grad_down[None])


def solution(mesh):
    placed = (
        P(("groups", "expert"), None),
        P(("groups", "expert"), None),
        P(("groups", "expert"), None),
        P("expert", None, None),
        P("expert", None, None),
        P(("groups", "expert"), None),
    )
    return jax.shard_map(
        on_device,
        mesh=mesh,
        in_specs=placed,
        out_specs=(
            P(("groups", "expert"), None),
            P(("groups", "expert"), None),
            P(("groups", "expert"), None, None),
            P(("groups", "expert"), None, None),
        ),
        check_vma=False,
    )
```

```python
import functools
import jax
import jax.numpy as jnp
from jax import lax
from jax.experimental import pallas as pl
from jax.experimental.pallas import tpu as pltpu
from jax.sharding import PartitionSpec as P

HEADS = 4
SPLIT = 4
VMEM = 20 * 1024 * 1024
FREE = pl.CostEstimate(flops=1, bytes_accessed=1, transcendentals=0)


def swap(value, bits, odd_bits=0):
    count = lax.axis_size("expert")
    return lax.ppermute(
        value, "expert", [(i, i ^ bits ^ (odd_bits if i % 2 else 0)) for i in range(count)]
    )


class Order:
    def __init__(self):
        self.last = ()

    def wait(self, *values):
        values = lax.optimization_barrier((*values, *self.last))[: len(values)]
        self.last = values[:1]
        return values[0] if len(values) == 1 else values

    def done(self, value):
        self.last = (*self.last, value)

    def now(self, value):
        return lax.optimization_barrier((value, *self.last))[0]

    def begin(self, send, value, *where):
        return send(self.now(value), *where)


def silu_grad(values):
    gate_sig = jax.nn.sigmoid(values)
    return gate_sig * (1.0 + values * (1.0 - gate_sig))


def heads_of(index, per_head):
    head = jnp.zeros_like(index)
    for h in range(1, HEADS):
        head = head + (index >= h * per_head).astype(jnp.int32)
    return head


def natural(index, per_head):
    head = heads_of(index, per_head)
    return HEADS * (index - per_head * head) + head


def iota(shape, dim):
    return lax.broadcasted_iota(jnp.int32, shape, dim)


def by_head(pair_rows):
    rows = pair_rows.shape[1]
    place = natural(iota((rows, rows), 1), rows // HEADS)
    turn = (iota((rows, rows), 0) == place).astype(jnp.float32)
    return jnp.dot(
        pair_rows, turn, preferred_element_type=jnp.float32, precision=lax.Precision.HIGHEST
    )


def ranks(me, routes_ref, experts_all):
    rows = routes_ref.shape[1]
    routes = by_head(routes_ref[...].astype(jnp.float32)).astype(jnp.int32)
    first, second = routes[0:1], routes[1:2]
    expert = iota((experts_all, rows), 0)
    named = ((expert == first) | (expert == second)).astype(jnp.bfloat16)
    earlier = (
        natural(iota((rows, rows), 0), rows // HEADS)
        < natural(iota((rows, rows), 1), rows // HEADS)
    ).astype(jnp.bfloat16)
    rank = jnp.dot(named, earlier, preferred_element_type=jnp.float32).astype(jnp.int32)
    return [
        (which ^ me, jnp.sum(jnp.where(expert == which, rank, 0), axis=0, keepdims=True))
        for which in (first, second)
    ]


def stacked(tokens_ref):
    feature = tokens_ref.shape[1] // HEADS
    return jnp.concatenate(
        [tokens_ref[:, h * feature : (h + 1) * feature] for h in range(HEADS)], axis=0
    )


def place_kernel(experts_all, capacity, gated, index_ref, *refs):
    routes_refs, refs = refs[:2], refs[2:]
    if gated:
        gates_refs, refs = refs[:2], refs[2:]
    tokens_refs, blocks = refs[:2], refs[2:]
    rows = routes_refs[0].shape[1]
    me, core = index_ref[0] // SPLIT, index_ref[0] % 2
    slot = iota((experts_all * capacity, rows), 0)
    picks, weight = [], 0.0
    for source in range(2):
        hits = []
        for distance, rank in ranks(me, routes_refs[source], experts_all):
            spot = ((distance >> 1) * 2 + source) * capacity + rank
            hits.append(slot == jnp.where((distance & 1) == core, spot, -1))
        picks.append((hits[0] | hits[1]).astype(jnp.bfloat16))
        if gated:
            gates = by_head(gates_refs[source][...])
            for k in range(2):
                weight = weight + jnp.where(hits[k], gates[k : k + 1], 0.0)
    placed = jnp.dot(
        jnp.concatenate(picks, axis=1),
        jnp.concatenate([stacked(ref) for ref in tokens_refs], axis=0),
        preferred_element_type=jnp.float32,
    )
    if gated:
        placed = jnp.sum(weight, axis=1, keepdims=True) * placed
    placed = placed.astype(jnp.bfloat16)
    for m, block in enumerate(blocks):
        block[...] = placed[2 * m * capacity : 2 * (m + 1) * capacity]


def column(row):
    count = row.shape[1]
    return jnp.sum(
        jnp.where(iota((count, count), 0) == iota((count, count), 1), row, jnp.zeros((), row.dtype)),
        axis=1,
        keepdims=True,
    )


def collect_kernel(experts_all, capacity, gated, index_ref, routes_ref, *refs):
    if gated:
        gates_ref, refs = refs[0], refs[1:]
    blocks, other_ref, out_ref = refs[:-2], refs[-2], refs[-1]
    rows = routes_ref.shape[1]
    feature = out_ref.shape[1] // HEADS
    me, core = index_ref[0] // SPLIT, index_ref[0] % 2
    values = jnp.concatenate([block[:capacity] for block in blocks] + [other_ref[...]], axis=0)
    slot = iota((rows, experts_all * capacity), 1)
    hits = []
    for distance, rank in ranks(me, routes_ref, experts_all):
        far = ((distance & 1) != core).astype(jnp.int32)
        spot = (far * (experts_all // 2) + (distance >> 1)) * capacity + rank
        hits.append(slot == column(spot))
    if gated:
        gates = by_head(gates_ref[...])
        total = sum(
            column(gates[k : k + 1])
            * jnp.dot(
                hits[k].astype(jnp.bfloat16), values, preferred_element_type=jnp.float32
            )
            for k in range(2)
        )
    else:
        total = jnp.dot(
            (hits[0] | hits[1]).astype(jnp.bfloat16), values, preferred_element_type=jnp.float32
        )
    total = total.astype(jnp.bfloat16)
    per_head = rows // HEADS
    for h in range(HEADS):
        out_ref[:, h * feature : (h + 1) * feature] = total[h * per_head : (h + 1) * per_head]


def place(index, routes, gates, tokens, experts_all, capacity):
    feature = tokens[0].shape[1] // HEADS
    operands = [*routes, *gates, *tokens]
    block = jax.ShapeDtypeStruct((2 * capacity, feature), jnp.bfloat16)
    return pl.pallas_call(
        functools.partial(place_kernel, experts_all, capacity, bool(gates)),
        out_shape=[block] * (experts_all // 2),
        in_specs=[pl.BlockSpec(memory_space=pltpu.SMEM)] + [pl.BlockSpec()] * len(operands),
        out_specs=[pl.BlockSpec(memory_space=pltpu.VMEM)] * (experts_all // 2),
        cost_estimate=FREE,
        compiler_params=pltpu.CompilerParams(vmem_limit_bytes=VMEM),
    )(index, *operands)


def collect(index, routes, gates, blocks, other, tok_local, experts_all, capacity):
    feature = other.shape[1]
    vmem = pl.BlockSpec(memory_space=pltpu.VMEM)
    operands = [routes, *gates, *blocks, other]
    return pl.pallas_call(
        functools.partial(collect_kernel, experts_all, capacity, bool(gates)),
        out_shape=jax.ShapeDtypeStruct((tok_local, HEADS * feature), jnp.bfloat16),
        in_specs=[pl.BlockSpec(memory_space=pltpu.SMEM)] + [vmem] * len(operands),
        out_specs=vmem,
        cost_estimate=FREE,
        compiler_params=pltpu.CompilerParams(vmem_limit_bytes=VMEM),
    )(index, *operands)


def dot(a, b, dims):
    return lax.dot_general(a, b, (dims, ((), ())), preferred_element_type=jnp.float32)


def call(kernel, out_shape, *operands):
    vmem = pl.BlockSpec(memory_space=pltpu.VMEM)
    return pl.pallas_call(
        kernel,
        out_shape=[jax.ShapeDtypeStruct(shape, dtype) for shape, dtype in out_shape],
        in_specs=[vmem] * len(operands),
        out_specs=[vmem] * len(out_shape),
        cost_estimate=FREE,
        compiler_params=pltpu.CompilerParams(vmem_limit_bytes=VMEM),
    )(*operands)


def forward_kernel(mine, far, up0, up1, down0, down1, pre0, pre1, hid0, hid1, part, part_far):
    rows = jnp.concatenate([mine[...], far[...]], axis=0)
    total = 0.0
    for up, down, pre, hid in ((up0, down0, pre0, hid0), (up1, down1, pre1, hid1)):
        act = dot(rows, up[...], ((1,), (0,)))
        pre[...] = act
        hidden = (act * jax.nn.sigmoid(act)).astype(jnp.bfloat16)
        hid[...] = hidden
        total = total + dot(hidden, down[...], ((1,), (0,)))
    total = total.astype(jnp.bfloat16)
    part[...] = total[: mine.shape[0]]
    part_far[...] = total[mine.shape[0] :]


def forward(mine, far, weights):
    rows, feature = mine.shape
    block = weights[0].shape[1]
    both = (2 * rows, block)
    pre0, pre1, hid0, hid1, part, part_far = call(
        forward_kernel,
        [(both, jnp.float32)] * 2 + [(both, jnp.bfloat16)] * 2 + [(mine.shape, jnp.bfloat16)] * 2,
        mine,
        far,
        *weights,
    )
    return (pre0, pre1), (hid0, hid1), part, part_far


def backward_kernel(mine, far, pre0, pre1, up0, up1, down0, down1, dpre0, dpre1, back, *backs_far):
    rows = jnp.concatenate([mine[...], far[...]], axis=0)
    total = 0.0
    for up, down, pre, dpre in ((up0, down0, pre0, dpre0), (up1, down1, pre1, dpre1)):
        grad = (dot(rows, down[...], ((1,), (1,))) * silu_grad(pre[...])).astype(jnp.bfloat16)
        dpre[...] = grad
        total = total + dot(grad, up[...], ((1,), (1,)))
    total = total.astype(jnp.bfloat16)
    back[...] = total[: mine.shape[0]]
    rows = backs_far[0].shape[0]
    for i, back_far in enumerate(backs_far):
        back_far[...] = total[mine.shape[0] + i * rows : mine.shape[0] + (i + 1) * rows]


def backward(mine, far, pre, weights, cuts=1):
    piece = (mine.shape[0] // cuts, mine.shape[1])
    dpre0, dpre1, *backs = call(
        backward_kernel,
        [(pre[0].shape, jnp.bfloat16)] * 2
        + [(mine.shape, jnp.bfloat16)]
        + [(piece, jnp.bfloat16)] * cuts,
        mine,
        far,
        *pre,
        *weights,
    )
    return (dpre0, dpre1), *backs


def add_kernel(first, mine, far, *outs):
    mine = mine[first : first + far.shape[0]]
    total = (mine.astype(jnp.float32) + far[...].astype(jnp.float32)).astype(jnp.bfloat16)
    rows = outs[0].shape[0]
    for i, out in enumerate(outs):
        out[...] = total[i * rows : (i + 1) * rows]


def added(mine, far, group, first=0):
    kernel = functools.partial(add_kernel, first * far.shape[0])
    shape = (far.shape[0] // len(group), mine.shape[1])
    return dict(zip(group, call(kernel, [(shape, jnp.bfloat16)] * len(group), mine, far)))


def weight_kernel(lefts, rights, others, *refs):
    both = lefts + rights
    left = jnp.concatenate([ref[...] for ref in refs[:lefts]], axis=0)
    right = jnp.concatenate([ref[...] for ref in refs[lefts:both]], axis=0)
    total = dot(left, right, ((0,), (0,)))
    if others:
        other = jnp.concatenate([ref[...] for ref in refs[both : both + others]], axis=0)
        total = total + other.astype(jnp.float32)
    outs = refs[both + others :]
    rows = outs[0].shape[0]
    for i, out in enumerate(outs):
        out[...] = total[i * rows : (i + 1) * rows].astype(out.dtype)


def weight_grad(dtype, cuts, left, right, others=()):
    shape = (left[0].shape[1] // cuts, right[0].shape[1])
    kernel = functools.partial(weight_kernel, len(left), len(right), len(others))
    return call(kernel, [(shape, dtype)] * cuts, *left, *right, *others)


def hop(value, line):
    return swap(value, 2 * SPLIT * line, SPLIT)


def on_device(tokens, routes, gates, w_up, w_down, cotangent):
    devices = lax.axis_size("expert")
    experts_all = devices // SPLIT
    tok_local = tokens.shape[0]
    capacity = SPLIT * (
        (6 * HEADS * tok_local + 2 * experts_all * SPLIT - 1) // (2 * experts_all * SPLIT)
    )
    capacity = 16 * ((capacity + 15) // 16)
    index = lax.axis_index("expert").astype(jnp.int32).reshape(1)
    lines = experts_all // 2
    cuts = [0, lines // 2, lines - lines // 4, lines]
    near, mid, far = (list(range(a, b)) for a, b in zip(cuts, cuts[1:]))

    def joined(blocks, group):
        return blocks[group[0]] if len(group) == 1 else jnp.concatenate([blocks[m] for m in group])

    order = Order()

    def hops(blocks, group):
        return {m: order.begin(hop, blocks[m], m) for m in group}

    def come(sent):
        return dict(zip(sent, jax.tree.leaves(order.wait(*sent.values()))))

    def across(value):
        return order.begin(swap, value, 2)

    def core(value):
        return order.begin(swap, value, 1)

    def halves(blocks):
        return jnp.concatenate([blocks[m][capacity:] for m in sorted(blocks)])

    def ordered(blocks):
        return [blocks[m] for m in sorted(blocks)]

    sizes = (tok_local, experts_all, capacity)
    up_own, down_own = w_up[0], w_down[0]
    routes, gates = routes.T, gates.T

    tokens_other, routes_other = order.wait(core(tokens), core(routes))
    routes_both = (routes, routes_other)
    x_blocks = place(index, routes_both, (), (tokens, tokens_other), experts_all, capacity)
    order.done(x_blocks[0])
    x_near, x_mid, x_far = hops(x_blocks, near), hops(x_blocks, mid), hops(x_blocks, far)
    up_other, down_other = core(up_own), core(down_own)
    x0 = joined(come(x_near), near)
    x0_far = across(x0)
    *x1, up_other, down_other = order.wait(*ordered(x_mid), up_other, down_other)
    weights = (up_own, up_other, down_own, down_other)
    x1 = joined(dict(zip(mid, x1)), mid)
    x1_far = across(x1)
    cotangent_other, gates_other = order.wait(core(cotangent), core(gates))
    g_blocks = place(
        index,
        routes_both,
        (gates, gates_other),
        (cotangent, cotangent_other),
        experts_all,
        capacity,
    )
    order.done(g_blocks[0])
    pre0, hid0, part0, part0_far = forward(x0, order.wait(x0_far), weights)
    order.done(part0_far)
    m0_far = across(part0_far)
    x2 = joined(come(x_far), far)
    x2_far, g_far = across(x2), hops(g_blocks, far)
    pre1, hid1, part1, part1_far = forward(x1, order.wait(x1_far), weights)
    order.done(part1_far)
    m1_far, g_mid = across(part1_far), hops(g_blocks, mid)
    pre2, hid2, part2, part2_far = forward(x2, order.wait(x2_far), weights)
    order.done(part2_far)
    m2_far = across(part2_far)

    m_sum = added(part0, order.wait(m0_far), near)
    order.done(m_sum[near[0]])
    g2 = joined(come(g_far), far)
    g2_far = across(g2)
    m_sum |= added(part1, order.wait(m1_far), mid)
    order.done(m_sum[mid[0]])
    g_near, m_mid = hops(g_blocks, near), hops(m_sum, mid)
    g1 = joined(come(g_mid), mid)
    g1_far = across(g1)
    m_sum |= added(part2, order.wait(m2_far), far)
    order.done(m_sum[far[0]])
    m_far = hops(m_sum, far)
    g0 = joined(come(g_near), near)
    g0_far = across(g0)
    dpre2, back2, back2_far = backward(g2, order.wait(g2_far), pre2, weights)
    order.done(back2_far)
    b2_far = across(back2_far)
    m_home = come(m_mid)
    dpre1, back1, back1_far = backward(g1, order.wait(g1_far), pre1, weights)
    order.done(back1_far)
    b1_far = across(back1_far)

    b_sum = added(back2, order.wait(b2_far), far)
    order.done(b_sum[far[0]])
    b_far = hops(b_sum, far)
    m_home |= come(m_far)
    b_sum |= added(back1, order.wait(b1_far), mid)
    order.done(b_sum[mid[0]])
    b_mid = hops(b_sum, mid)
    dpre0, back0, back0_far = backward(g0, order.wait(g0_far), pre0, weights)
    order.done(back0_far)
    b0_far = across(back0_far)
    b_home = come(b_far)
    m_late = hops(m_sum, near)
    m_home |= come({m: m_late[m] for m in near[:1]})

    x_all = (x0, x0_far, x1, x1_far, x2, x2_far)
    g_all = (g0, g0_far, g1, g1_far, g2, g2_far)
    hid_own, hid_other = zip(hid0, hid1, hid2)
    dpre_own, dpre_other = zip(dpre0, dpre1, dpre2)
    down_part = weight_grad(jnp.bfloat16, 2, (order.now(hid0[1]), *hid_other[1:]), g_all)
    up_part = weight_grad(jnp.bfloat16, 2, x_all, (order.now(dpre0[1]), *dpre_other[1:]))
    order.done(down_part[0])
    order.done(up_part[0])
    b_home |= come(b_mid)
    m_home |= come({m: m_late[m] for m in near[1:]})
    m_other = core(halves(m_home))
    b_sum |= added(back0, order.wait(b0_far), near)
    order.done(b_sum[near[0]])
    b_near = hops(b_sum, near)
    down_sent, up_sent = [core(part) for part in down_part], [core(part) for part in up_part]
    mixed = collect(index, routes, (gates,), ordered(m_home), order.wait(m_other), *sizes)
    order.done(mixed)
    b_home |= come(b_near)
    b_other = core(halves(b_home))
    (grad_down,) = weight_grad(jnp.float32, 1, hid_own, g_all, order.wait(*down_sent))
    order.done(grad_down)
    (grad_up,) = weight_grad(jnp.float32, 1, x_all, dpre_own, order.wait(*up_sent))
    order.done(grad_up)
    b_other = order.wait(b_other)
    token_grad = collect(index, routes, (), ordered(b_home), b_other, *sizes)
    return (mixed, token_grad, grad_up[None], grad_down[None])


def solution(mesh):
    placed = (
        P(("groups", "expert"), None),
        P(("groups", "expert"), None),
        P(("groups", "expert"), None),
        P("expert", None, None),
        P("expert", None, None),
        P(("groups", "expert"), None),
    )
    return jax.shard_map(
        on_device,
        mesh=mesh,
        in_specs=placed,
        out_specs=(
            P(("groups", "expert"), None),
            P(("groups", "expert"), None),
            P(("groups", "expert"), None, None),
            P(("groups", "expert"), None, None),
        ),
        check_vma=False,
    )
```

```python
import functools
import jax
import jax.numpy as jnp
from jax import lax
from jax.experimental import pallas as pl
from jax.experimental.pallas import tpu as pltpu
from jax.sharding import PartitionSpec as P

HEADS = 4
SPLIT = 4
VMEM = 20 * 1024 * 1024
FREE = pl.CostEstimate(flops=1, bytes_accessed=1, transcendentals=0)


def swap(value, bits, odd_bits=0):
    count = lax.axis_size("expert")
    return lax.ppermute(
        value, "expert", [(i, i ^ bits ^ (odd_bits if i % 2 else 0)) for i in range(count)]
    )


class Order:
    def __init__(self):
        self.last = ()

    def wait(self, *values):
        values = lax.optimization_barrier((*values, *self.last))[: len(values)]
        self.last = values[:1]
        return values[0] if len(values) == 1 else values

    def done(self, value):
        self.last = (*self.last, value)

    def now(self, value):
        return lax.optimization_barrier((value, *self.last))[0]

    def begin(self, send, value, *where):
        return send(self.now(value), *where)


def silu_grad(values):
    gate_sig = jax.nn.sigmoid(values)
    return gate_sig * (1.0 + values * (1.0 - gate_sig))


def heads_of(index, per_head):
    head = jnp.zeros_like(index)
    for h in range(1, HEADS):
        head = head + (index >= h * per_head).astype(jnp.int32)
    return head


def natural(index, per_head):
    head = heads_of(index, per_head)
    return HEADS * (index - per_head * head) + head


def iota(shape, dim):
    return lax.broadcasted_iota(jnp.int32, shape, dim)


def by_head(pair_rows):
    rows = pair_rows.shape[1]
    place = natural(iota((rows, rows), 1), rows // HEADS)
    turn = (iota((rows, rows), 0) == place).astype(jnp.float32)
    return jnp.dot(
        pair_rows, turn, preferred_element_type=jnp.float32, precision=lax.Precision.HIGHEST
    )


def ranks(me, routes_ref, experts_all):
    rows = routes_ref.shape[1]
    routes = by_head(routes_ref[...].astype(jnp.float32)).astype(jnp.int32)
    first, second = routes[0:1], routes[1:2]
    expert = iota((experts_all, rows), 0)
    named = ((expert == first) | (expert == second)).astype(jnp.bfloat16)
    earlier = (
        natural(iota((rows, rows), 0), rows // HEADS)
        < natural(iota((rows, rows), 1), rows // HEADS)
    ).astype(jnp.bfloat16)
    rank = jnp.dot(named, earlier, preferred_element_type=jnp.float32).astype(jnp.int32)
    return [
        (which ^ me, jnp.sum(jnp.where(expert == which, rank, 0), axis=0, keepdims=True))
        for which in (first, second)
    ]


def stacked(tokens_ref):
    feature = tokens_ref.shape[1] // HEADS
    return jnp.concatenate(
        [tokens_ref[:, h * feature : (h + 1) * feature] for h in range(HEADS)], axis=0
    )


def place_kernel(experts_all, capacity, gated, index_ref, *refs):
    routes_refs, refs = refs[:2], refs[2:]
    if gated:
        gates_refs, refs = refs[:2], refs[2:]
    tokens_refs, blocks = refs[:2], refs[2:]
    rows = routes_refs[0].shape[1]
    me, core = index_ref[0] // SPLIT, index_ref[0] % 2
    slot = iota((experts_all * capacity, rows), 0)
    picks, weight = [], 0.0
    for source in range(2):
        hits = []
        for distance, rank in ranks(me, routes_refs[source], experts_all):
            spot = ((distance >> 1) * 2 + source) * capacity + rank
            hits.append(slot == jnp.where((distance & 1) == core, spot, -1))
        picks.append((hits[0] | hits[1]).astype(jnp.bfloat16))
        if gated:
            gates = by_head(gates_refs[source][...])
            for k in range(2):
                weight = weight + jnp.where(hits[k], gates[k : k + 1], 0.0)
    placed = jnp.dot(
        jnp.concatenate(picks, axis=1),
        jnp.concatenate([stacked(ref) for ref in tokens_refs], axis=0),
        preferred_element_type=jnp.float32,
    )
    if gated:
        placed = jnp.sum(weight, axis=1, keepdims=True) * placed
    placed = placed.astype(jnp.bfloat16)
    for m, block in enumerate(blocks):
        block[...] = placed[2 * m * capacity : 2 * (m + 1) * capacity]


def column(row):
    count = row.shape[1]
    return jnp.sum(
        jnp.where(iota((count, count), 0) == iota((count, count), 1), row, jnp.zeros((), row.dtype)),
        axis=1,
        keepdims=True,
    )


def collect_kernel(experts_all, capacity, gated, index_ref, routes_ref, *refs):
    if gated:
        gates_ref, refs = refs[0], refs[1:]
    lines = experts_all // 2
    blocks, others, out_ref = refs[:lines], refs[lines:-1], refs[-1]
    rows = routes_ref.shape[1]
    feature = out_ref.shape[1] // HEADS
    me, core = index_ref[0] // SPLIT, index_ref[0] % 2
    values = jnp.concatenate([block[:capacity] for block in blocks] + [other[...] for other in others], axis=0)
    slot = iota((rows, experts_all * capacity), 1)
    hits = []
    for distance, rank in ranks(me, routes_ref, experts_all):
        far = ((distance & 1) != core).astype(jnp.int32)
        spot = (far * (experts_all // 2) + (distance >> 1)) * capacity + rank
        hits.append(slot == column(spot))
    if gated:
        gates = by_head(gates_ref[...])
        total = sum(
            column(gates[k : k + 1])
            * jnp.dot(
                hits[k].astype(jnp.bfloat16), values, preferred_element_type=jnp.float32
            )
            for k in range(2)
        )
    else:
        total = jnp.dot(
            (hits[0] | hits[1]).astype(jnp.bfloat16), values, preferred_element_type=jnp.float32
        )
    total = total.astype(jnp.bfloat16)
    per_head = rows // HEADS
    for h in range(HEADS):
        out_ref[:, h * feature : (h + 1) * feature] = total[h * per_head : (h + 1) * per_head]


def place(index, routes, gates, tokens, experts_all, capacity):
    feature = tokens[0].shape[1] // HEADS
    operands = [*routes, *gates, *tokens]
    block = jax.ShapeDtypeStruct((2 * capacity, feature), jnp.bfloat16)
    return pl.pallas_call(
        functools.partial(place_kernel, experts_all, capacity, bool(gates)),
        out_shape=[block] * (experts_all // 2),
        in_specs=[pl.BlockSpec(memory_space=pltpu.SMEM)] + [pl.BlockSpec()] * len(operands),
        out_specs=[pl.BlockSpec(memory_space=pltpu.VMEM)] * (experts_all // 2),
        cost_estimate=FREE,
        compiler_params=pltpu.CompilerParams(vmem_limit_bytes=VMEM),
    )(index, *operands)


def collect(index, routes, gates, blocks, others, tok_local, experts_all, capacity):
    feature = blocks[0].shape[1]
    vmem = pl.BlockSpec(memory_space=pltpu.VMEM)
    operands = [routes, *gates, *blocks, *others]
    return pl.pallas_call(
        functools.partial(collect_kernel, experts_all, capacity, bool(gates)),
        out_shape=jax.ShapeDtypeStruct((tok_local, HEADS * feature), jnp.bfloat16),
        in_specs=[pl.BlockSpec(memory_space=pltpu.SMEM)] + [vmem] * len(operands),
        out_specs=vmem,
        cost_estimate=FREE,
        compiler_params=pltpu.CompilerParams(vmem_limit_bytes=VMEM),
    )(index, *operands)


def dot(a, b, dims):
    return lax.dot_general(a, b, (dims, ((), ())), preferred_element_type=jnp.float32)


def call(kernel, out_shape, *operands):
    vmem = pl.BlockSpec(memory_space=pltpu.VMEM)
    return pl.pallas_call(
        kernel,
        out_shape=[jax.ShapeDtypeStruct(shape, dtype) for shape, dtype in out_shape],
        in_specs=[vmem] * len(operands),
        out_specs=[vmem] * len(out_shape),
        cost_estimate=FREE,
        compiler_params=pltpu.CompilerParams(vmem_limit_bytes=VMEM),
    )(*operands)


def forward_kernel(mine, far, up0, up1, down0, down1, pre0, pre1, hid0, hid1, part, part_far):
    rows = jnp.concatenate([mine[...], far[...]], axis=0)
    total = 0.0
    for up, down, pre, hid in ((up0, down0, pre0, hid0), (up1, down1, pre1, hid1)):
        act = dot(rows, up[...], ((1,), (0,)))
        pre[...] = act
        hidden = (act * jax.nn.sigmoid(act)).astype(jnp.bfloat16)
        hid[...] = hidden
        total = total + dot(hidden, down[...], ((1,), (0,)))
    total = total.astype(jnp.bfloat16)
    part[...] = total[: mine.shape[0]]
    part_far[...] = total[mine.shape[0] :]


def forward(mine, far, weights):
    rows, feature = mine.shape
    block = weights[0].shape[1]
    both = (2 * rows, block)
    pre0, pre1, hid0, hid1, part, part_far = call(
        forward_kernel,
        [(both, jnp.float32)] * 2 + [(both, jnp.bfloat16)] * 2 + [(mine.shape, jnp.bfloat16)] * 2,
        mine,
        far,
        *weights,
    )
    return (pre0, pre1), (hid0, hid1), part, part_far


def backward_kernel(mine, far, pre0, pre1, up0, up1, down0, down1, dpre0, dpre1, back, *backs_far):
    rows = jnp.concatenate([mine[...], far[...]], axis=0)
    total = 0.0
    for up, down, pre, dpre in ((up0, down0, pre0, dpre0), (up1, down1, pre1, dpre1)):
        grad = (dot(rows, down[...], ((1,), (1,))) * silu_grad(pre[...])).astype(jnp.bfloat16)
        dpre[...] = grad
        total = total + dot(grad, up[...], ((1,), (1,)))
    total = total.astype(jnp.bfloat16)
    back[...] = total[: mine.shape[0]]
    rows = backs_far[0].shape[0]
    for i, back_far in enumerate(backs_far):
        back_far[...] = total[mine.shape[0] + i * rows : mine.shape[0] + (i + 1) * rows]


def backward(mine, far, pre, weights, cuts=1):
    piece = (mine.shape[0] // cuts, mine.shape[1])
    dpre0, dpre1, *backs = call(
        backward_kernel,
        [(pre[0].shape, jnp.bfloat16)] * 2
        + [(mine.shape, jnp.bfloat16)]
        + [(piece, jnp.bfloat16)] * cuts,
        mine,
        far,
        *pre,
        *weights,
    )
    return (dpre0, dpre1), *backs


def add_kernel(first, mine, far, *outs):
    mine = mine[first : first + far.shape[0]]
    total = (mine.astype(jnp.float32) + far[...].astype(jnp.float32)).astype(jnp.bfloat16)
    rows = outs[0].shape[0]
    for i, out in enumerate(outs):
        out[...] = total[i * rows : (i + 1) * rows]


def added(mine, far, group, first=0):
    kernel = functools.partial(add_kernel, first * far.shape[0])
    shape = (far.shape[0] // len(group), mine.shape[1])
    return dict(zip(group, call(kernel, [(shape, jnp.bfloat16)] * len(group), mine, far)))


def weight_kernel(lefts, rights, *refs):
    left = jnp.concatenate([ref[...] for ref in refs[:lefts]], axis=0)
    right = jnp.concatenate([ref[...] for ref in refs[lefts : lefts + rights]], axis=0)
    total = dot(left, right, ((0,), (0,)))
    outs = refs[lefts + rights :]
    rows = outs[0].shape[0]
    for i, out in enumerate(outs):
        out[...] = total[i * rows : (i + 1) * rows].astype(out.dtype)


def weight_grad(dtype, cuts, left, right):
    shape = (left[0].shape[1] // cuts, right[0].shape[1])
    kernel = functools.partial(weight_kernel, len(left), len(right))
    return call(kernel, [(shape, dtype)] * cuts, *left, *right)


def joined_kernel(own, other, out):
    out[...] = own[...] + other[...].astype(jnp.float32)


def joined_weights(own, other):
    return call(joined_kernel, [(own.shape, jnp.float32)], own, other)[0]


def hop(value, line):
    return swap(value, 2 * SPLIT * line, SPLIT)


def on_device(tokens, routes, gates, w_up, w_down, cotangent):
    devices = lax.axis_size("expert")
    experts_all = devices // SPLIT
    tok_local = tokens.shape[0]
    capacity = SPLIT * (
        (6 * HEADS * tok_local + 2 * experts_all * SPLIT - 1) // (2 * experts_all * SPLIT)
    )
    capacity = 16 * ((capacity + 15) // 16)
    index = lax.axis_index("expert").astype(jnp.int32).reshape(1)
    lines = experts_all // 2
    cuts = [0, lines // 2, lines - lines // 4, lines]
    near, mid, far = (list(range(a, b)) for a, b in zip(cuts, cuts[1:]))

    def joined(blocks, group):
        return blocks[group[0]] if len(group) == 1 else jnp.concatenate([blocks[m] for m in group])

    order = Order()

    def hops(blocks, group):
        return {m: order.begin(hop, blocks[m], m) for m in group}

    def come(sent):
        return dict(zip(sent, jax.tree.leaves(order.wait(*sent.values()))))

    def across(value):
        return order.begin(swap, value, 2)

    def core(value):
        return order.begin(swap, value, 1)

    def halves(blocks):
        return jnp.concatenate([blocks[m][capacity:] for m in sorted(blocks)])

    def ordered(blocks):
        return [blocks[m] for m in sorted(blocks)]

    sizes = (tok_local, experts_all, capacity)
    up_own, down_own = w_up[0], w_down[0]
    routes, gates = routes.T, gates.T

    tokens_other, routes_other = order.wait(core(tokens), core(routes))
    routes_both = (routes, routes_other)
    x_blocks = place(index, routes_both, (), (tokens, tokens_other), experts_all, capacity)
    order.done(x_blocks[0])
    x_near, x_mid, x_far = hops(x_blocks, near), hops(x_blocks, mid), hops(x_blocks, far)
    up_other, down_other = core(up_own), core(down_own)
    x0 = joined(come(x_near), near)
    x0_far = across(x0)
    *x1, up_other, down_other = order.wait(*ordered(x_mid), up_other, down_other)
    weights = (up_own, up_other, down_own, down_other)
    x1 = joined(dict(zip(mid, x1)), mid)
    x1_far = across(x1)
    cotangent_other, gates_other = order.wait(core(cotangent), core(gates))
    g_blocks = place(
        index,
        routes_both,
        (gates, gates_other),
        (cotangent, cotangent_other),
        experts_all,
        capacity,
    )
    order.done(g_blocks[0])
    pre0, hid0, part0, part0_far = forward(x0, order.wait(x0_far), weights)
    order.done(part0_far)
    m0_far = across(part0_far)
    x2 = joined(come(x_far), far)
    x2_far, g_far = across(x2), hops(g_blocks, far)
    pre1, hid1, part1, part1_far = forward(x1, order.wait(x1_far), weights)
    order.done(part1_far)
    m1_far, g_mid = across(part1_far), hops(g_blocks, mid)
    pre2, hid2, part2, part2_far = forward(x2, order.wait(x2_far), weights)
    order.done(part2_far)
    m2_far = across(part2_far)

    m_sum = added(part0, order.wait(m0_far), near)
    order.done(m_sum[near[0]])
    g2 = joined(come(g_far), far)
    g2_far = across(g2)
    m_sum |= added(part1, order.wait(m1_far), mid)
    order.done(m_sum[mid[0]])
    g_near, m_mid = hops(g_blocks, near), hops(m_sum, mid)
    g1 = joined(come(g_mid), mid)
    g1_far = across(g1)
    m_sum |= added(part2, order.wait(m2_far), far)
    order.done(m_sum[far[0]])
    m_far = hops(m_sum, far)
    g0 = joined(come(g_near), near)
    g0_far = across(g0)
    dpre2, back2, back2_far = backward(g2, order.wait(g2_far), pre2, weights)
    order.done(back2_far)
    b2_far = across(back2_far)
    m_home = come(m_mid)
    dpre1, back1, back1_far = backward(g1, order.wait(g1_far), pre1, weights)
    order.done(back1_far)
    b1_far = across(back1_far)

    b_sum = added(back2, order.wait(b2_far), far)
    order.done(b_sum[far[0]])
    b_far = hops(b_sum, far)
    m_home |= come(m_far)
    m_near = hops(m_sum, near)
    b_sum |= added(back1, order.wait(b1_far), mid)
    order.done(b_sum[mid[0]])
    b_mid = hops(b_sum, mid)
    dpre0, back0, back0_far = backward(g0, order.wait(g0_far), pre0, weights)
    order.done(back0_far)
    b0_far = across(back0_far)
    b_home = come(b_far)
    m_other = order.wait(core(halves(m_home)))

    x_all = (x0, x0_far, x1, x1_far, x2, x2_far)
    g_all = (g0, g0_far, g1, g1_far, g2, g2_far)
    hid_own, hid_other = zip(hid0, hid1, hid2)
    dpre_own, dpre_other = zip(dpre0, dpre1, dpre2)
    (down_part,) = weight_grad(jnp.bfloat16, 1, (order.now(hid0[1]), *hid_other[1:]), g_all)
    (up_part,) = weight_grad(jnp.bfloat16, 1, x_all, (order.now(dpre0[1]), *dpre_other[1:]))
    order.done(down_part)
    order.done(up_part)
    (down_own_part,) = weight_grad(jnp.float32, 1, (order.now(hid0[0]), *hid_own[1:]), g_all)
    order.done(down_own_part)
    (up_own_part,) = weight_grad(jnp.float32, 1, x_all, (order.now(dpre0[0]), *dpre_own[1:]))
    order.done(up_own_part)
    down_sent, up_sent = core(down_part), core(up_part)
    b_home |= come(b_mid)
    m_near = come(m_near)
    m_near_other = core(halves(m_near))
    b_sum |= added(back0, order.wait(b0_far), near)
    order.done(b_sum[near[0]])
    b_near = hops(b_sum, near)
    mixed = collect(
        index,
        routes,
        (gates,),
        ordered(m_home | m_near),
        [order.wait(m_near_other), m_other],
        *sizes,
    )
    order.done(mixed)
    b_home |= come(b_near)
    b_other = core(halves(b_home))
    grad_down = joined_weights(down_own_part, order.wait(down_sent))
    order.done(grad_down)
    grad_up = joined_weights(up_own_part, order.wait(up_sent))
    order.done(grad_up)
    b_other = order.wait(b_other)
    token_grad = collect(index, routes, (), ordered(b_home), [b_other], *sizes)
    return (mixed, token_grad, grad_up[None], grad_down[None])


def solution(mesh):
    placed = (
        P(("groups", "expert"), None),
        P(("groups", "expert"), None),
        P(("groups", "expert"), None),
        P("expert", None, None),
        P("expert", None, None),
        P(("groups", "expert"), None),
    )
    return jax.shard_map(
        on_device,
        mesh=mesh,
        in_specs=placed,
        out_specs=(
            P(("groups", "expert"), None),
            P(("groups", "expert"), None),
            P(("groups", "expert"), None, None),
            P(("groups", "expert"), None, None),
        ),
        check_vma=False,
    )
```

```python
import functools
import jax
import jax.numpy as jnp
from jax import lax
from jax.experimental import pallas as pl
from jax.experimental.pallas import tpu as pltpu
from jax.sharding import PartitionSpec as P

HEADS = 4
SPLIT = 4
VMEM = 20 * 1024 * 1024
FREE = pl.CostEstimate(flops=1, bytes_accessed=1, transcendentals=0)


def swap(value, bits, odd_bits=0):
    count = lax.axis_size("expert")
    return lax.ppermute(
        value, "expert", [(i, i ^ bits ^ (odd_bits if i % 2 else 0)) for i in range(count)]
    )


class Order:
    def __init__(self):
        self.last = ()

    def wait(self, *values):
        values = lax.optimization_barrier((*values, *self.last))[: len(values)]
        self.last = values[:1]
        return values[0] if len(values) == 1 else values

    def done(self, value):
        self.last = (*self.last, value)

    def now(self, value):
        return lax.optimization_barrier((value, *self.last))[0]

    def begin(self, send, value, *where):
        return send(self.now(value), *where)


def silu_grad(values):
    gate_sig = jax.nn.sigmoid(values)
    return gate_sig * (1.0 + values * (1.0 - gate_sig))


def heads_of(index, per_head):
    head = jnp.zeros_like(index)
    for h in range(1, HEADS):
        head = head + (index >= h * per_head).astype(jnp.int32)
    return head


def natural(index, per_head):
    head = heads_of(index, per_head)
    return HEADS * (index - per_head * head) + head


def iota(shape, dim):
    return lax.broadcasted_iota(jnp.int32, shape, dim)


def by_head(pair_rows):
    rows = pair_rows.shape[1]
    place = natural(iota((rows, rows), 1), rows // HEADS)
    turn = (iota((rows, rows), 0) == place).astype(jnp.float32)
    return jnp.dot(
        pair_rows, turn, preferred_element_type=jnp.float32, precision=lax.Precision.HIGHEST
    )


def ranks(me, routes_ref, experts_all):
    rows = routes_ref.shape[1]
    routes = by_head(routes_ref[...].astype(jnp.float32)).astype(jnp.int32)
    first, second = routes[0:1], routes[1:2]
    expert = iota((experts_all, rows), 0)
    named = ((expert == first) | (expert == second)).astype(jnp.bfloat16)
    earlier = (
        natural(iota((rows, rows), 0), rows // HEADS)
        < natural(iota((rows, rows), 1), rows // HEADS)
    ).astype(jnp.bfloat16)
    rank = jnp.dot(named, earlier, preferred_element_type=jnp.float32).astype(jnp.int32)
    return [
        (which ^ me, jnp.sum(jnp.where(expert == which, rank, 0), axis=0, keepdims=True))
        for which in (first, second)
    ]


def stacked(tokens_ref):
    feature = tokens_ref.shape[1] // HEADS
    return jnp.concatenate(
        [tokens_ref[:, h * feature : (h + 1) * feature] for h in range(HEADS)], axis=0
    )


def place_kernel(experts_all, capacity, gated, index_ref, *refs):
    routes_refs, refs = refs[:2], refs[2:]
    if gated:
        gates_refs, refs = refs[:2], refs[2:]
    tokens_refs, blocks = refs[:2], refs[-(experts_all // 2) :]
    rows = routes_refs[0].shape[1]
    me, core = index_ref[0] // SPLIT, index_ref[0] % 2
    slot = iota((experts_all * capacity, rows), 0)
    picks, weight = [], 0.0
    for source in range(2):
        hits = []
        for distance, rank in ranks(me, routes_refs[source], experts_all):
            spot = ((distance >> 1) * 2 + source) * capacity + rank
            hits.append(slot == jnp.where((distance & 1) == core, spot, -1))
        picks.append((hits[0] | hits[1]).astype(jnp.bfloat16))
        if gated:
            gates = by_head(gates_refs[source][...])
            for k in range(2):
                weight = weight + jnp.where(hits[k], gates[k : k + 1], 0.0)
    placed = jnp.dot(
        jnp.concatenate(picks, axis=1),
        jnp.concatenate([stacked(ref) for ref in tokens_refs], axis=0),
        preferred_element_type=jnp.float32,
    )
    if gated:
        placed = jnp.sum(weight, axis=1, keepdims=True) * placed
    placed = placed.astype(jnp.bfloat16)
    for m, block in enumerate(blocks):
        block[...] = placed[2 * m * capacity : 2 * (m + 1) * capacity]


def column(row):
    count = row.shape[1]
    return jnp.sum(
        jnp.where(iota((count, count), 0) == iota((count, count), 1), row, jnp.zeros((), row.dtype)),
        axis=1,
        keepdims=True,
    )


def collect_kernel(experts_all, capacity, gated, index_ref, routes_ref, *refs):
    if gated:
        gates_ref, refs = refs[0], refs[1:]
    lines = experts_all // 2
    blocks, others, out_ref = refs[:lines], refs[lines:-1], refs[-1]
    rows = routes_ref.shape[1]
    feature = out_ref.shape[1] // HEADS
    me, core = index_ref[0] // SPLIT, index_ref[0] % 2
    values = jnp.concatenate([block[:capacity] for block in blocks] + [other[...] for other in others], axis=0)
    slot = iota((rows, experts_all * capacity), 1)
    hits = []
    for distance, rank in ranks(me, routes_ref, experts_all):
        far = ((distance & 1) != core).astype(jnp.int32)
        spot = (far * (experts_all // 2) + (distance >> 1)) * capacity + rank
        hits.append(slot == column(spot))
    if gated:
        gates = by_head(gates_ref[...])
        total = sum(
            column(gates[k : k + 1])
            * jnp.dot(
                hits[k].astype(jnp.bfloat16), values, preferred_element_type=jnp.float32
            )
            for k in range(2)
        )
    else:
        total = jnp.dot(
            (hits[0] | hits[1]).astype(jnp.bfloat16), values, preferred_element_type=jnp.float32
        )
    total = total.astype(jnp.bfloat16)
    per_head = rows // HEADS
    for h in range(HEADS):
        out_ref[:, h * feature : (h + 1) * feature] = total[h * per_head : (h + 1) * per_head]


def place(index, routes, gates, tokens, experts_all, capacity, *ahead):
    feature = tokens[0].shape[1] // HEADS
    operands = [*routes, *gates, *tokens]
    vmem = pl.BlockSpec(memory_space=pltpu.VMEM)
    block = jax.ShapeDtypeStruct((2 * capacity, feature), jnp.bfloat16)
    return pl.pallas_call(
        functools.partial(place_kernel, experts_all, capacity, bool(gates)),
        out_shape=[block] * (experts_all // 2),
        in_specs=[pl.BlockSpec(memory_space=pltpu.SMEM)] + [pl.BlockSpec()] * len(operands)
        + [vmem] * len(ahead),
        out_specs=[vmem] * (experts_all // 2),
        cost_estimate=FREE,
        compiler_params=pltpu.CompilerParams(vmem_limit_bytes=VMEM),
    )(index, *operands, *ahead)


def collect(index, routes, gates, blocks, others, tok_local, experts_all, capacity):
    feature = blocks[0].shape[1]
    vmem = pl.BlockSpec(memory_space=pltpu.VMEM)
    operands = [routes, *gates, *blocks, *others]
    return pl.pallas_call(
        functools.partial(collect_kernel, experts_all, capacity, bool(gates)),
        out_shape=jax.ShapeDtypeStruct((tok_local, HEADS * feature), jnp.bfloat16),
        in_specs=[pl.BlockSpec(memory_space=pltpu.SMEM)] + [vmem] * len(operands),
        out_specs=vmem,
        cost_estimate=FREE,
        compiler_params=pltpu.CompilerParams(vmem_limit_bytes=VMEM),
    )(index, *operands)


def dot(a, b, dims):
    return lax.dot_general(a, b, (dims, ((), ())), preferred_element_type=jnp.float32)


def call(kernel, out_shape, *operands):
    vmem = pl.BlockSpec(memory_space=pltpu.VMEM)
    return pl.pallas_call(
        kernel,
        out_shape=[jax.ShapeDtypeStruct(shape, dtype) for shape, dtype in out_shape],
        in_specs=[vmem] * len(operands),
        out_specs=[vmem] * len(out_shape),
        cost_estimate=FREE,
        compiler_params=pltpu.CompilerParams(vmem_limit_bytes=VMEM),
    )(*operands)


def forward_kernel(mine, far, up0, up1, down0, down1, pre0, pre1, hid0, hid1, part, part_far):
    rows = jnp.concatenate([mine[...], far[...]], axis=0)
    total = 0.0
    for up, down, pre, hid in ((up0, down0, pre0, hid0), (up1, down1, pre1, hid1)):
        act = dot(rows, up[...], ((1,), (0,)))
        pre[...] = act
        hidden = (act * jax.nn.sigmoid(act)).astype(jnp.bfloat16)
        hid[...] = hidden
        total = total + dot(hidden, down[...], ((1,), (0,)))
    total = total.astype(jnp.bfloat16)
    part[...] = total[: mine.shape[0]]
    part_far[...] = total[mine.shape[0] :]


def forward(mine, far, weights):
    rows, feature = mine.shape
    block = weights[0].shape[1]
    both = (2 * rows, block)
    pre0, pre1, hid0, hid1, part, part_far = call(
        forward_kernel,
        [(both, jnp.float32)] * 2 + [(both, jnp.bfloat16)] * 2 + [(mine.shape, jnp.bfloat16)] * 2,
        mine,
        far,
        *weights,
    )
    return (pre0, pre1), (hid0, hid1), part, part_far


def backward_kernel(mine, far, pre0, pre1, up0, up1, down0, down1, dpre0, dpre1, back, *backs_far):
    rows = jnp.concatenate([mine[...], far[...]], axis=0)
    total = 0.0
    for up, down, pre, dpre in ((up0, down0, pre0, dpre0), (up1, down1, pre1, dpre1)):
        grad = (dot(rows, down[...], ((1,), (1,))) * silu_grad(pre[...])).astype(jnp.bfloat16)
        dpre[...] = grad
        total = total + dot(grad, up[...], ((1,), (1,)))
    total = total.astype(jnp.bfloat16)
    back[...] = total[: mine.shape[0]]
    rows = backs_far[0].shape[0]
    for i, back_far in enumerate(backs_far):
        back_far[...] = total[mine.shape[0] + i * rows : mine.shape[0] + (i + 1) * rows]


def backward(mine, far, pre, weights, cuts=1):
    piece = (mine.shape[0] // cuts, mine.shape[1])
    dpre0, dpre1, *backs = call(
        backward_kernel,
        [(pre[0].shape, jnp.bfloat16)] * 2
        + [(mine.shape, jnp.bfloat16)]
        + [(piece, jnp.bfloat16)] * cuts,
        mine,
        far,
        *pre,
        *weights,
    )
    return (dpre0, dpre1), *backs


def add_kernel(first, mine, far, *outs):
    mine = mine[first : first + far.shape[0]]
    total = (mine.astype(jnp.float32) + far[...].astype(jnp.float32)).astype(jnp.bfloat16)
    rows = outs[0].shape[0]
    for i, out in enumerate(outs):
        out[...] = total[i * rows : (i + 1) * rows]


def added(mine, far, group, first=0):
    kernel = functools.partial(add_kernel, first * far.shape[0])
    shape = (far.shape[0] // len(group), mine.shape[1])
    return dict(zip(group, call(kernel, [(shape, jnp.bfloat16)] * len(group), mine, far)))


def weight_kernel(lefts, rights, *refs):
    left = jnp.concatenate([ref[...] for ref in refs[:lefts]], axis=0)
    right = jnp.concatenate([ref[...] for ref in refs[lefts : lefts + rights]], axis=0)
    total = dot(left, right, ((0,), (0,)))
    outs = refs[lefts + rights :]
    rows = outs[0].shape[0]
    for i, out in enumerate(outs):
        out[...] = total[i * rows : (i + 1) * rows].astype(out.dtype)


def weight_grad(dtype, cuts, left, right):
    shape = (left[0].shape[1] // cuts, right[0].shape[1])
    kernel = functools.partial(weight_kernel, len(left), len(right))
    return call(kernel, [(shape, dtype)] * cuts, *left, *right)


def joined_kernel(own, other, out):
    out[...] = own[...] + other[...].astype(jnp.float32)


def joined_weights(own, other):
    return call(joined_kernel, [(own.shape, jnp.float32)], own, other)[0]


def hop(value, line):
    return swap(value, 2 * SPLIT * line, SPLIT)


def on_device(tokens, routes, gates, w_up, w_down, cotangent):
    devices = lax.axis_size("expert")
    experts_all = devices // SPLIT
    tok_local = tokens.shape[0]
    capacity = SPLIT * (
        (6 * HEADS * tok_local + 2 * experts_all * SPLIT - 1) // (2 * experts_all * SPLIT)
    )
    capacity = 16 * ((capacity + 15) // 16)
    index = lax.axis_index("expert").astype(jnp.int32).reshape(1)
    lines = experts_all // 2
    cuts = [0, lines // 2, lines - lines // 4, lines]
    near, mid, far = (list(range(a, b)) for a, b in zip(cuts, cuts[1:]))

    def joined(blocks, group):
        return blocks[group[0]] if len(group) == 1 else jnp.concatenate([blocks[m] for m in group])

    order = Order()

    def hops(blocks, group):
        return {m: order.begin(hop, blocks[m], m) for m in group}

    def come(sent):
        return dict(zip(sent, jax.tree.leaves(order.wait(*sent.values()))))

    def across(value):
        return order.begin(swap, value, 2)

    def core(value):
        return order.begin(swap, value, 1)

    def halves(blocks):
        return jnp.concatenate([blocks[m][capacity:] for m in sorted(blocks)])

    def ordered(blocks):
        return [blocks[m] for m in sorted(blocks)]

    sizes = (tok_local, experts_all, capacity)
    up_own, down_own = w_up[0], w_down[0]
    routes, gates = routes.T, gates.T

    tokens_other, routes_other = order.wait(core(tokens), core(routes))
    routes_both = (routes, routes_other)
    x_blocks = place(index, routes_both, (), (tokens, tokens_other), experts_all, capacity)
    order.done(x_blocks[0])
    x_near, x_mid, x_far = hops(x_blocks, near), hops(x_blocks, mid), hops(x_blocks, far)
    up_other, down_other = core(up_own), core(down_own)
    x0 = joined(come(x_near), near)
    x0_far = across(x0)
    *x1, up_other, down_other = order.wait(*ordered(x_mid), up_other, down_other)
    weights = (up_own, up_other, down_own, down_other)
    x1 = joined(dict(zip(mid, x1)), mid)
    x1_far = across(x1)
    cotangent_other, gates_other = order.wait(core(cotangent), core(gates))
    g_blocks = place(
        index,
        routes_both,
        (gates, gates_other),
        (cotangent, cotangent_other),
        experts_all,
        capacity,
        up_own,
        down_own,
    )
    order.done(g_blocks[0])
    pre0, hid0, part0, part0_far = forward(x0, order.wait(x0_far), weights)
    order.done(part0_far)
    m0_far = across(part0_far)
    x2 = joined(come(x_far), far)
    x2_far, g_far = across(x2), hops(g_blocks, far)
    pre1, hid1, part1, part1_far = forward(x1, order.wait(x1_far), weights)
    order.done(part1_far)
    m1_far, g_mid = across(part1_far), hops(g_blocks, mid)
    pre2, hid2, part2, part2_far = forward(x2, order.wait(x2_far), weights)
    order.done(part2_far)
    m2_far = across(part2_far)

    m_sum = added(part0, order.wait(m0_far), near)
    order.done(m_sum[near[0]])
    g2 = joined(come(g_far), far)
    g2_far = across(g2)
    m_sum |= added(part1, order.wait(m1_far), mid)
    order.done(m_sum[mid[0]])
    g_near, m_mid = hops(g_blocks, near), hops(m_sum, mid)
    g1 = joined(come(g_mid), mid)
    g1_far = across(g1)
    m_sum |= added(part2, order.wait(m2_far), far)
    order.done(m_sum[far[0]])
    m_far = hops(m_sum, far)
    g0 = joined(come(g_near), near)
    g0_far = across(g0)
    dpre2, back2, back2_far = backward(g2, order.wait(g2_far), pre2, weights)
    order.done(back2_far)
    b2_far = across(back2_far)
    m_home = come(m_mid)
    dpre1, back1, back1_far = backward(g1, order.wait(g1_far), pre1, weights)
    order.done(back1_far)
    b1_far = across(back1_far)

    b_sum = added(back2, order.wait(b2_far), far)
    order.done(b_sum[far[0]])
    b_far = hops(b_sum, far)
    m_home |= come(m_far)
    m_near = hops(m_sum, near)
    b_sum |= added(back1, order.wait(b1_far), mid)
    order.done(b_sum[mid[0]])
    b_mid = hops(b_sum, mid)
    dpre0, back0, back0_far = backward(g0, order.wait(g0_far), pre0, weights)
    order.done(back0_far)
    b0_far = across(back0_far)
    b_home = come(b_far)
    m_other = order.wait(core(halves(m_home)))

    x_all = (x0, x0_far, x1, x1_far, x2, x2_far)
    g_all = (g0, g0_far, g1, g1_far, g2, g2_far)
    hid_own, hid_other = zip(hid0, hid1, hid2)
    dpre_own, dpre_other = zip(dpre0, dpre1, dpre2)
    (down_part,) = weight_grad(jnp.bfloat16, 1, (order.now(hid0[1]), *hid_other[1:]), g_all)
    (up_part,) = weight_grad(jnp.bfloat16, 1, x_all, (order.now(dpre0[1]), *dpre_other[1:]))
    order.done(down_part)
    order.done(up_part)
    (down_own_part,) = weight_grad(jnp.float32, 1, (order.now(hid0[0]), *hid_own[1:]), g_all)
    order.done(down_own_part)
    (up_own_part,) = weight_grad(jnp.float32, 1, x_all, (order.now(dpre0[0]), *dpre_own[1:]))
    order.done(up_own_part)
    down_sent, up_sent = core(down_part), core(up_part)
    b_home |= come(b_mid)
    m_near = come(m_near)
    m_near_other = core(halves(m_near))
    b_sum |= added(back0, order.wait(b0_far), near)
    order.done(b_sum[near[0]])
    b_near = hops(b_sum, near)
    mixed = collect(
        index,
        routes,
        (gates,),
        ordered(m_home | m_near),
        [order.wait(m_near_other), m_other],
        *sizes,
    )
    order.done(mixed)
    b_home |= come(b_near)
    b_other = core(halves(b_home))
    grad_down = joined_weights(down_own_part, order.wait(down_sent))
    order.done(grad_down)
    grad_up = joined_weights(up_own_part, order.wait(up_sent))
    order.done(grad_up)
    b_other = order.wait(b_other)
    token_grad = collect(index, routes, (), ordered(b_home), [b_other], *sizes)
    return (mixed, token_grad, grad_up[None], grad_down[None])


def solution(mesh):
    placed = (
        P(("groups", "expert"), None),
        P(("groups", "expert"), None),
        P(("groups", "expert"), None),
        P("expert", None, None),
        P("expert", None, None),
        P(("groups", "expert"), None),
    )
    return jax.shard_map(
        on_device,
        mesh=mesh,
        in_specs=placed,
        out_specs=(
            P(("groups", "expert"), None),
            P(("groups", "expert"), None),
            P(("groups", "expert"), None, None),
            P(("groups", "expert"), None, None),
        ),
        check_vma=False,
    )
```

```python
import functools
import jax
import jax.numpy as jnp
from jax import lax
from jax.experimental import pallas as pl
from jax.experimental.pallas import tpu as pltpu
from jax.sharding import PartitionSpec as P

HEADS = 4
SPLIT = 4
VMEM = 30 * 1024 * 1024
FREE = pl.CostEstimate(flops=1, bytes_accessed=1, transcendentals=0)


def swap(value, bits, odd_bits=0):
    count = lax.axis_size("expert")
    return lax.ppermute(
        value, "expert", [(i, i ^ bits ^ (odd_bits if i % 2 else 0)) for i in range(count)]
    )


class Order:
    def __init__(self):
        self.last = ()

    def wait(self, *values):
        values = lax.optimization_barrier((*values, *self.last))[: len(values)]
        self.last = values[:1]
        return values[0] if len(values) == 1 else values

    def done(self, value):
        self.last = (*self.last, value)

    def now(self, value):
        return lax.optimization_barrier((value, *self.last))[0]

    def begin(self, send, value, *where):
        return send(self.now(value), *where)


def silu_grad(values):
    gate_sig = jax.nn.sigmoid(values)
    return gate_sig * (1.0 + values * (1.0 - gate_sig))


def heads_of(index, per_head):
    head = jnp.zeros_like(index)
    for h in range(1, HEADS):
        head = head + (index >= h * per_head).astype(jnp.int32)
    return head


def natural(index, per_head):
    head = heads_of(index, per_head)
    return HEADS * (index - per_head * head) + head


def iota(shape, dim):
    return lax.broadcasted_iota(jnp.int32, shape, dim)


def by_head(pair_rows):
    rows = pair_rows.shape[1]
    place = natural(iota((rows, rows), 1), rows // HEADS)
    turn = (iota((rows, rows), 0) == place).astype(jnp.float32)
    return jnp.dot(
        pair_rows, turn, preferred_element_type=jnp.float32, precision=lax.Precision.HIGHEST
    )


def ranks(me, routes_ref, experts_all):
    rows = routes_ref.shape[1]
    routes = by_head(routes_ref[...].astype(jnp.float32)).astype(jnp.int32)
    first, second = routes[0:1], routes[1:2]
    expert = iota((experts_all, rows), 0)
    named = ((expert == first) | (expert == second)).astype(jnp.bfloat16)
    earlier = (
        natural(iota((rows, rows), 0), rows // HEADS)
        < natural(iota((rows, rows), 1), rows // HEADS)
    ).astype(jnp.bfloat16)
    rank = jnp.dot(named, earlier, preferred_element_type=jnp.float32).astype(jnp.int32)
    return [
        (which ^ me, jnp.sum(jnp.where(expert == which, rank, 0), axis=0, keepdims=True))
        for which in (first, second)
    ]


def stacked(tokens_ref):
    feature = tokens_ref.shape[1] // HEADS
    return jnp.concatenate(
        [tokens_ref[:, h * feature : (h + 1) * feature] for h in range(HEADS)], axis=0
    )


def place_kernel(experts_all, capacity, gated, index_ref, *refs):
    routes_refs, refs = refs[:2], refs[2:]
    if gated:
        gates_refs, refs = refs[:2], refs[2:]
    tokens_refs, blocks = refs[:2], refs[-(experts_all // 2) :]
    rows = routes_refs[0].shape[1]
    me, core = index_ref[0] // SPLIT, index_ref[0] % 2
    slot = iota((experts_all * capacity, rows), 0)
    picks, weight = [], 0.0
    for source in range(2):
        hits = []
        for distance, rank in ranks(me, routes_refs[source], experts_all):
            spot = ((distance >> 1) * 2 + source) * capacity + rank
            hits.append(slot == jnp.where((distance & 1) == core, spot, -1))
        picks.append((hits[0] | hits[1]).astype(jnp.bfloat16))
        if gated:
            gates = by_head(gates_refs[source][...])
            for k in range(2):
                weight = weight + jnp.where(hits[k], gates[k : k + 1], 0.0)
    placed = jnp.dot(
        jnp.concatenate(picks, axis=1),
        jnp.concatenate([stacked(ref) for ref in tokens_refs], axis=0),
        preferred_element_type=jnp.float32,
    )
    if gated:
        placed = jnp.sum(weight, axis=1, keepdims=True) * placed
    placed = placed.astype(jnp.bfloat16)
    for m, block in enumerate(blocks):
        block[...] = placed[2 * m * capacity : 2 * (m + 1) * capacity]


def column(row):
    count = row.shape[1]
    return jnp.sum(
        jnp.where(iota((count, count), 0) == iota((count, count), 1), row, jnp.zeros((), row.dtype)),
        axis=1,
        keepdims=True,
    )


def collect_kernel(experts_all, capacity, gated, index_ref, routes_ref, *refs):
    if gated:
        gates_ref, refs = refs[0], refs[1:]
    lines = experts_all // 2
    blocks, others, out_ref = refs[:lines], refs[lines:-1], refs[-1]
    rows = routes_ref.shape[1]
    feature = out_ref.shape[1] // HEADS
    me, core = index_ref[0] // SPLIT, index_ref[0] % 2
    values = jnp.concatenate([block[:capacity] for block in blocks] + [other[...] for other in others], axis=0)
    slot = iota((rows, experts_all * capacity), 1)
    hits = []
    for distance, rank in ranks(me, routes_ref, experts_all):
        far = ((distance & 1) != core).astype(jnp.int32)
        spot = (far * (experts_all // 2) + (distance >> 1)) * capacity + rank
        hits.append(slot == column(spot))
    if gated:
        gates = by_head(gates_ref[...])
        total = sum(
            column(gates[k : k + 1])
            * jnp.dot(
                hits[k].astype(jnp.bfloat16), values, preferred_element_type=jnp.float32
            )
            for k in range(2)
        )
    else:
        total = jnp.dot(
            (hits[0] | hits[1]).astype(jnp.bfloat16), values, preferred_element_type=jnp.float32
        )
    total = total.astype(jnp.bfloat16)
    per_head = rows // HEADS
    for h in range(HEADS):
        out_ref[:, h * feature : (h + 1) * feature] = total[h * per_head : (h + 1) * per_head]


def place(index, routes, gates, tokens, experts_all, capacity, *ahead):
    feature = tokens[0].shape[1] // HEADS
    operands = [*routes, *gates, *tokens]
    vmem = pl.BlockSpec(memory_space=pltpu.VMEM)
    block = jax.ShapeDtypeStruct((2 * capacity, feature), jnp.bfloat16)
    return pl.pallas_call(
        functools.partial(place_kernel, experts_all, capacity, bool(gates)),
        out_shape=[block] * (experts_all // 2),
        in_specs=[pl.BlockSpec(memory_space=pltpu.SMEM)] + [pl.BlockSpec()] * len(operands)
        + [vmem] * len(ahead),
        out_specs=[vmem] * (experts_all // 2),
        cost_estimate=FREE,
        compiler_params=pltpu.CompilerParams(vmem_limit_bytes=VMEM),
    )(index, *operands, *ahead)


def collect(index, routes, gates, blocks, others, tok_local, experts_all, capacity):
    feature = blocks[0].shape[1]
    vmem = pl.BlockSpec(memory_space=pltpu.VMEM)
    operands = [routes, *gates, *blocks, *others]
    return pl.pallas_call(
        functools.partial(collect_kernel, experts_all, capacity, bool(gates)),
        out_shape=jax.ShapeDtypeStruct((tok_local, HEADS * feature), jnp.bfloat16),
        in_specs=[pl.BlockSpec(memory_space=pltpu.SMEM)] + [vmem] * len(operands),
        out_specs=vmem,
        cost_estimate=FREE,
        compiler_params=pltpu.CompilerParams(vmem_limit_bytes=VMEM),
    )(index, *operands)


def dot(a, b, dims):
    return lax.dot_general(a, b, (dims, ((), ())), preferred_element_type=jnp.float32)


def call(kernel, out_shape, *operands):
    vmem = pl.BlockSpec(memory_space=pltpu.VMEM)
    return pl.pallas_call(
        kernel,
        out_shape=[jax.ShapeDtypeStruct(shape, dtype) for shape, dtype in out_shape],
        in_specs=[vmem] * len(operands),
        out_specs=[vmem] * len(out_shape),
        cost_estimate=FREE,
        compiler_params=pltpu.CompilerParams(vmem_limit_bytes=VMEM),
    )(*operands)


def forward_kernel(mine, far, up0, up1, down0, down1, pre0, pre1, hid0, hid1, part, part_far):
    rows = jnp.concatenate([mine[...], far[...]], axis=0)
    total = 0.0
    for up, down, pre, hid in ((up0, down0, pre0, hid0), (up1, down1, pre1, hid1)):
        act = dot(rows, up[...], ((1,), (0,)))
        pre[...] = act
        hidden = (act * jax.nn.sigmoid(act)).astype(jnp.bfloat16)
        hid[...] = hidden
        total = total + dot(hidden, down[...], ((1,), (0,)))
    total = total.astype(jnp.bfloat16)
    part[...] = total[: mine.shape[0]]
    part_far[...] = total[mine.shape[0] :]


def forward(mine, far, weights):
    rows, feature = mine.shape
    block = weights[0].shape[1]
    both = (2 * rows, block)
    pre0, pre1, hid0, hid1, part, part_far = call(
        forward_kernel,
        [(both, jnp.float32)] * 2 + [(both, jnp.bfloat16)] * 2 + [(mine.shape, jnp.bfloat16)] * 2,
        mine,
        far,
        *weights,
    )
    return (pre0, pre1), (hid0, hid1), part, part_far


def backward_kernel(mine, far, pre0, pre1, up0, up1, down0, down1, dpre0, dpre1, back, *backs_far):
    rows = jnp.concatenate([mine[...], far[...]], axis=0)
    total = 0.0
    for up, down, pre, dpre in ((up0, down0, pre0, dpre0), (up1, down1, pre1, dpre1)):
        grad = (dot(rows, down[...], ((1,), (1,))) * silu_grad(pre[...])).astype(jnp.bfloat16)
        dpre[...] = grad
        total = total + dot(grad, up[...], ((1,), (1,)))
    total = total.astype(jnp.bfloat16)
    back[...] = total[: mine.shape[0]]
    rows = backs_far[0].shape[0]
    for i, back_far in enumerate(backs_far):
        back_far[...] = total[mine.shape[0] + i * rows : mine.shape[0] + (i + 1) * rows]


def backward(mine, far, pre, weights, cuts=1):
    piece = (mine.shape[0] // cuts, mine.shape[1])
    dpre0, dpre1, *backs = call(
        backward_kernel,
        [(pre[0].shape, jnp.bfloat16)] * 2
        + [(mine.shape, jnp.bfloat16)]
        + [(piece, jnp.bfloat16)] * cuts,
        mine,
        far,
        *pre,
        *weights,
    )
    return (dpre0, dpre1), *backs


def add_kernel(first, mine, far, *outs):
    mine = mine[first : first + far.shape[0]]
    total = (mine.astype(jnp.float32) + far[...].astype(jnp.float32)).astype(jnp.bfloat16)
    rows = outs[0].shape[0]
    for i, out in enumerate(outs):
        out[...] = total[i * rows : (i + 1) * rows]


def added(mine, far, group, first=0):
    kernel = functools.partial(add_kernel, first * far.shape[0])
    shape = (far.shape[0] // len(group), mine.shape[1])
    return dict(zip(group, call(kernel, [(shape, jnp.bfloat16)] * len(group), mine, far)))


def weight_kernel(lefts, rights, *refs):
    left = jnp.concatenate([ref[...] for ref in refs[:lefts]], axis=0)
    right = jnp.concatenate([ref[...] for ref in refs[lefts : lefts + rights]], axis=0)
    total = dot(left, right, ((0,), (0,)))
    outs = refs[lefts + rights :]
    rows = outs[0].shape[0]
    for i, out in enumerate(outs):
        out[...] = total[i * rows : (i + 1) * rows].astype(out.dtype)


def weight_grad(dtype, cuts, left, right):
    shape = (left[0].shape[1] // cuts, right[0].shape[1])
    kernel = functools.partial(weight_kernel, len(left), len(right))
    return call(kernel, [(shape, dtype)] * cuts, *left, *right)


def joined_kernel(own, *refs):
    out = refs[-1]
    rows = refs[0].shape[0]
    for i, ref in enumerate(refs[:-1]):
        part = slice(i * rows, (i + 1) * rows)
        out[part] = own[part] + ref[...].astype(jnp.float32)


def joined_weights(own, pieces):
    return call(joined_kernel, [(own.shape, jnp.float32)], own, *pieces)[0]


def hop(value, line):
    return swap(value, 2 * SPLIT * line, SPLIT)


def on_device(tokens, routes, gates, w_up, w_down, cotangent):
    devices = lax.axis_size("expert")
    experts_all = devices // SPLIT
    tok_local = tokens.shape[0]
    capacity = SPLIT * (
        (6 * HEADS * tok_local + 2 * experts_all * SPLIT - 1) // (2 * experts_all * SPLIT)
    )
    capacity = 16 * ((capacity + 15) // 16)
    index = lax.axis_index("expert").astype(jnp.int32).reshape(1)
    lines = experts_all // 2
    cuts = [0, lines // 2, lines - lines // 4, lines]
    near, mid, far = (list(range(a, b)) for a, b in zip(cuts, cuts[1:]))

    def joined(blocks, group):
        return blocks[group[0]] if len(group) == 1 else jnp.concatenate([blocks[m] for m in group])

    order = Order()

    def hops(blocks, group):
        return {m: order.begin(hop, blocks[m], m) for m in group}

    def come(sent):
        return dict(zip(sent, jax.tree.leaves(order.wait(*sent.values()))))

    def across(value):
        return order.begin(swap, value, 2)

    def core(value):
        return order.begin(swap, value, 1)

    def halves(blocks):
        return jnp.concatenate([blocks[m][capacity:] for m in sorted(blocks)])

    def ordered(blocks):
        return [blocks[m] for m in sorted(blocks)]

    sizes = (tok_local, experts_all, capacity)
    up_own, down_own = w_up[0], w_down[0]
    routes, gates = routes.T, gates.T

    tokens_other, routes_other = order.wait(core(tokens), core(routes))
    routes_both = (routes, routes_other)
    x_blocks = place(index, routes_both, (), (tokens, tokens_other), experts_all, capacity)
    order.done(x_blocks[0])
    x_near, x_mid, x_far = hops(x_blocks, near), hops(x_blocks, mid), hops(x_blocks, far)
    up_other, down_other = core(up_own), core(down_own)
    x0 = joined(come(x_near), near)
    x0_far = across(x0)
    *x1, up_other, down_other = order.wait(*ordered(x_mid), up_other, down_other)
    weights = (up_own, up_other, down_own, down_other)
    x1 = joined(dict(zip(mid, x1)), mid)
    x1_far = across(x1)
    cotangent_other, gates_other = order.wait(core(cotangent), core(gates))
    g_blocks = place(
        index,
        routes_both,
        (gates, gates_other),
        (cotangent, cotangent_other),
        experts_all,
        capacity,
        up_own,
        down_own,
    )
    order.done(g_blocks[0])
    pre0, hid0, part0, part0_far = forward(x0, order.wait(x0_far), weights)
    order.done(part0_far)
    m0_far = across(part0_far)
    x2 = joined(come(x_far), far)
    x2_far, g_far = across(x2), hops(g_blocks, far)
    pre1, hid1, part1, part1_far = forward(x1, order.wait(x1_far), weights)
    order.done(part1_far)
    m1_far, g_mid = across(part1_far), hops(g_blocks, mid)
    pre2, hid2, part2, part2_far = forward(x2, order.wait(x2_far), weights)
    order.done(part2_far)
    m2_far = across(part2_far)

    m_sum = added(part0, order.wait(m0_far), near)
    order.done(m_sum[near[0]])
    g2 = joined(come(g_far), far)
    g2_far = across(g2)
    m_sum |= added(part1, order.wait(m1_far), mid)
    order.done(m_sum[mid[0]])
    g_near, m_mid = hops(g_blocks, near), hops(m_sum, mid)
    g1 = joined(come(g_mid), mid)
    g1_far = across(g1)
    m_sum |= added(part2, order.wait(m2_far), far)
    order.done(m_sum[far[0]])
    m_far = hops(m_sum, far)
    g0 = joined(come(g_near), near)
    g0_far = across(g0)
    dpre2, back2, back2_far = backward(g2, order.wait(g2_far), pre2, weights)
    order.done(back2_far)
    b2_far = across(back2_far)
    m_home = come(m_mid)
    dpre1, back1, back1_far = backward(g1, order.wait(g1_far), pre1, weights)
    order.done(back1_far)
    b1_far = across(back1_far)

    b_sum = added(back2, order.wait(b2_far), far)
    order.done(b_sum[far[0]])
    b_far = hops(b_sum, far)
    m_home |= come(m_far)
    m_near = hops(m_sum, near)
    b_sum |= added(back1, order.wait(b1_far), mid)
    order.done(b_sum[mid[0]])
    b_mid = hops(b_sum, mid)
    dpre0, back0, back0_far = backward(g0, order.wait(g0_far), pre0, weights)
    order.done(back0_far)
    b0_far = across(back0_far)
    b_home = come(b_far)
    m_other = order.wait(core(halves(m_home)))

    x_all = (x0, x0_far, x1, x1_far, x2, x2_far)
    g_all = (g0, g0_far, g1, g1_far, g2, g2_far)
    hid_own, hid_other = zip(hid0, hid1, hid2)
    dpre_own, dpre_other = zip(dpre0, dpre1, dpre2)
    down_part = weight_grad(jnp.bfloat16, 2, (order.now(hid0[1]), *hid_other[1:]), g_all)
    up_part = weight_grad(jnp.bfloat16, 2, x_all, (order.now(dpre0[1]), *dpre_other[1:]))
    order.done(down_part[0])
    order.done(up_part[0])
    (down_own_part,) = weight_grad(jnp.float32, 1, (order.now(hid0[0]), *hid_own[1:]), g_all)
    order.done(down_own_part)
    (up_own_part,) = weight_grad(jnp.float32, 1, x_all, (order.now(dpre0[0]), *dpre_own[1:]))
    order.done(up_own_part)
    down_sent, up_sent = [core(part) for part in down_part], [core(part) for part in up_part]
    b_home |= come(b_mid)
    m_near = come(m_near)
    m_near_other = core(halves(m_near))
    b_sum |= added(back0, order.wait(b0_far), near)
    order.done(b_sum[near[0]])
    b_near = hops(b_sum, near)
    mixed = collect(
        index,
        routes,
        (gates,),
        ordered(m_home | m_near),
        [order.wait(m_near_other), m_other],
        *sizes,
    )
    order.done(mixed)
    grad_down = joined_weights(down_own_part, order.wait(*down_sent))
    order.done(grad_down)
    b_home |= come(b_near)
    b_other = core(halves(b_home))
    grad_up = joined_weights(up_own_part, order.wait(*up_sent))
    order.done(grad_up)
    b_other = order.wait(b_other)
    token_grad = collect(index, routes, (), ordered(b_home), [b_other], *sizes)
    return (mixed, token_grad, grad_up[None], grad_down[None])


def solution(mesh):
    placed = (
        P(("groups", "expert"), None),
        P(("groups", "expert"), None),
        P(("groups", "expert"), None),
        P("expert", None, None),
        P("expert", None, None),
        P(("groups", "expert"), None),
    )
    return jax.shard_map(
        on_device,
        mesh=mesh,
        in_specs=placed,
        out_specs=(
            P(("groups", "expert"), None),
            P(("groups", "expert"), None),
            P(("groups", "expert"), None, None),
            P(("groups", "expert"), None, None),
        ),
        check_vma=False,
    )
```

```python
import functools
import jax
import jax.numpy as jnp
from jax import lax
from jax.experimental import pallas as pl
from jax.experimental.pallas import tpu as pltpu
from jax.sharding import PartitionSpec as P

HEADS = 4
SPLIT = 4
VMEM = 30 * 1024 * 1024
FREE = pl.CostEstimate(flops=1, bytes_accessed=1, transcendentals=0)


def swap(value, bits, odd_bits=0):
    count = lax.axis_size("expert")
    return lax.ppermute(
        value, "expert", [(i, i ^ bits ^ (odd_bits if i % 2 else 0)) for i in range(count)]
    )


class Order:
    def __init__(self):
        self.last = ()

    def wait(self, *values):
        values = lax.optimization_barrier((*values, *self.last))[: len(values)]
        self.last = values[:1]
        return values[0] if len(values) == 1 else values

    def done(self, value):
        self.last = (*self.last, value)

    def now(self, value):
        return lax.optimization_barrier((value, *self.last))[0]

    def begin(self, send, value, *where):
        return send(self.now(value), *where)


def silu_grad(values):
    gate_sig = jax.nn.sigmoid(values)
    return gate_sig * (1.0 + values * (1.0 - gate_sig))


def heads_of(index, per_head):
    head = jnp.zeros_like(index)
    for h in range(1, HEADS):
        head = head + (index >= h * per_head).astype(jnp.int32)
    return head


def natural(index, per_head):
    head = heads_of(index, per_head)
    return HEADS * (index - per_head * head) + head


def iota(shape, dim):
    return lax.broadcasted_iota(jnp.int32, shape, dim)


def by_head(pair_rows):
    rows = pair_rows.shape[1]
    place = natural(iota((rows, rows), 1), rows // HEADS)
    turn = (iota((rows, rows), 0) == place).astype(jnp.float32)
    return jnp.dot(
        pair_rows, turn, preferred_element_type=jnp.float32, precision=lax.Precision.HIGHEST
    )


def ranks(me, routes_ref, experts_all):
    rows = routes_ref.shape[1]
    routes = by_head(routes_ref[...].astype(jnp.float32)).astype(jnp.int32)
    first, second = routes[0:1], routes[1:2]
    expert = iota((experts_all, rows), 0)
    named = ((expert == first) | (expert == second)).astype(jnp.bfloat16)
    earlier = (
        natural(iota((rows, rows), 0), rows // HEADS)
        < natural(iota((rows, rows), 1), rows // HEADS)
    ).astype(jnp.bfloat16)
    rank = jnp.dot(named, earlier, preferred_element_type=jnp.float32).astype(jnp.int32)
    return [
        (which ^ me, jnp.sum(jnp.where(expert == which, rank, 0), axis=0, keepdims=True))
        for which in (first, second)
    ]


def stacked(tokens_ref):
    feature = tokens_ref.shape[1] // HEADS
    return jnp.concatenate(
        [tokens_ref[:, h * feature : (h + 1) * feature] for h in range(HEADS)], axis=0
    )


def place_kernel(experts_all, capacity, gated, index_ref, *refs):
    routes_refs, refs = refs[:2], refs[2:]
    if gated:
        gates_refs, refs = refs[:2], refs[2:]
    tokens_refs, blocks = refs[:2], refs[-(experts_all // 2) :]
    rows = routes_refs[0].shape[1]
    me, core = index_ref[0] // SPLIT, index_ref[0] % 2
    slot = iota((experts_all * capacity, rows), 0)
    picks, weight = [], 0.0
    for source in range(2):
        hits = []
        for distance, rank in ranks(me, routes_refs[source], experts_all):
            spot = ((distance >> 1) * 2 + source) * capacity + rank
            hits.append(slot == jnp.where((distance & 1) == core, spot, -1))
        picks.append((hits[0] | hits[1]).astype(jnp.bfloat16))
        if gated:
            gates = by_head(gates_refs[source][...])
            for k in range(2):
                weight = weight + jnp.where(hits[k], gates[k : k + 1], 0.0)
    placed = jnp.dot(
        jnp.concatenate(picks, axis=1),
        jnp.concatenate([stacked(ref) for ref in tokens_refs], axis=0),
        preferred_element_type=jnp.float32,
    )
    if gated:
        placed = jnp.sum(weight, axis=1, keepdims=True) * placed
    placed = placed.astype(jnp.bfloat16)
    for m, block in enumerate(blocks):
        block[...] = placed[2 * m * capacity : 2 * (m + 1) * capacity]


def column(row):
    count = row.shape[1]
    return jnp.sum(
        jnp.where(iota((count, count), 0) == iota((count, count), 1), row, jnp.zeros((), row.dtype)),
        axis=1,
        keepdims=True,
    )


def collect_kernel(experts_all, capacity, gated, index_ref, routes_ref, *refs):
    if gated:
        gates_ref, refs = refs[0], refs[1:]
    lines = experts_all // 2
    blocks, others, out_ref = refs[:lines], refs[lines:-1], refs[-1]
    rows = routes_ref.shape[1]
    feature = out_ref.shape[1] // HEADS
    me, core = index_ref[0] // SPLIT, index_ref[0] % 2
    values = jnp.concatenate([block[:capacity] for block in blocks] + [other[...] for other in others], axis=0)
    slot = iota((rows, experts_all * capacity), 1)
    hits = []
    for distance, rank in ranks(me, routes_ref, experts_all):
        far = ((distance & 1) != core).astype(jnp.int32)
        spot = (far * (experts_all // 2) + (distance >> 1)) * capacity + rank
        hits.append(slot == column(spot))
    if gated:
        gates = by_head(gates_ref[...])
        total = sum(
            column(gates[k : k + 1])
            * jnp.dot(
                hits[k].astype(jnp.bfloat16), values, preferred_element_type=jnp.float32
            )
            for k in range(2)
        )
    else:
        total = jnp.dot(
            (hits[0] | hits[1]).astype(jnp.bfloat16), values, preferred_element_type=jnp.float32
        )
    total = total.astype(jnp.bfloat16)
    per_head = rows // HEADS
    for h in range(HEADS):
        out_ref[:, h * feature : (h + 1) * feature] = total[h * per_head : (h + 1) * per_head]


def place(index, routes, gates, tokens, experts_all, capacity, *ahead):
    feature = tokens[0].shape[1] // HEADS
    operands = [*routes, *gates, *tokens]
    vmem = pl.BlockSpec(memory_space=pltpu.VMEM)
    block = jax.ShapeDtypeStruct((2 * capacity, feature), jnp.bfloat16)
    return pl.pallas_call(
        functools.partial(place_kernel, experts_all, capacity, bool(gates)),
        out_shape=[block] * (experts_all // 2),
        in_specs=[pl.BlockSpec(memory_space=pltpu.SMEM)] + [pl.BlockSpec()] * len(operands)
        + [vmem] * len(ahead),
        out_specs=[vmem] * (experts_all // 2),
        cost_estimate=FREE,
        compiler_params=pltpu.CompilerParams(vmem_limit_bytes=VMEM),
    )(index, *operands, *ahead)


def collect(index, routes, gates, blocks, others, tok_local, experts_all, capacity):
    feature = blocks[0].shape[1]
    vmem = pl.BlockSpec(memory_space=pltpu.VMEM)
    operands = [routes, *gates, *blocks, *others]
    return pl.pallas_call(
        functools.partial(collect_kernel, experts_all, capacity, bool(gates)),
        out_shape=jax.ShapeDtypeStruct((tok_local, HEADS * feature), jnp.bfloat16),
        in_specs=[pl.BlockSpec(memory_space=pltpu.SMEM)] + [vmem] * len(operands),
        out_specs=vmem,
        cost_estimate=FREE,
        compiler_params=pltpu.CompilerParams(vmem_limit_bytes=VMEM),
    )(index, *operands)


def dot(a, b, dims):
    return lax.dot_general(a, b, (dims, ((), ())), preferred_element_type=jnp.float32)


def call(kernel, out_shape, *operands):
    vmem = pl.BlockSpec(memory_space=pltpu.VMEM)
    return pl.pallas_call(
        kernel,
        out_shape=[jax.ShapeDtypeStruct(shape, dtype) for shape, dtype in out_shape],
        in_specs=[vmem] * len(operands),
        out_specs=[vmem] * len(out_shape),
        cost_estimate=FREE,
        compiler_params=pltpu.CompilerParams(vmem_limit_bytes=VMEM),
    )(*operands)


def forward_kernel(mine, far, up0, up1, down0, down1, pre0, pre1, hid0, hid1, part, part_far):
    rows = jnp.concatenate([mine[...], far[...]], axis=0)
    total = 0.0
    for up, down, pre, hid in ((up0, down0, pre0, hid0), (up1, down1, pre1, hid1)):
        act = dot(rows, up[...], ((1,), (0,)))
        pre[...] = act
        hidden = (act * jax.nn.sigmoid(act)).astype(jnp.bfloat16)
        hid[...] = hidden
        total = total + dot(hidden, down[...], ((1,), (0,)))
    total = total.astype(jnp.bfloat16)
    part[...] = total[: mine.shape[0]]
    part_far[...] = total[mine.shape[0] :]


def forward(mine, far, weights):
    rows, feature = mine.shape
    block = weights[0].shape[1]
    both = (2 * rows, block)
    pre0, pre1, hid0, hid1, part, part_far = call(
        forward_kernel,
        [(both, jnp.float32)] * 2 + [(both, jnp.bfloat16)] * 2 + [(mine.shape, jnp.bfloat16)] * 2,
        mine,
        far,
        *weights,
    )
    return (pre0, pre1), (hid0, hid1), part, part_far


def backward_kernel(mine, far, pre0, pre1, up0, up1, down0, down1, dpre0, dpre1, back, *backs_far):
    rows = jnp.concatenate([mine[...], far[...]], axis=0)
    total = 0.0
    for up, down, pre, dpre in ((up0, down0, pre0, dpre0), (up1, down1, pre1, dpre1)):
        grad = (dot(rows, down[...], ((1,), (1,))) * silu_grad(pre[...])).astype(jnp.bfloat16)
        dpre[...] = grad
        total = total + dot(grad, up[...], ((1,), (1,)))
    total = total.astype(jnp.bfloat16)
    back[...] = total[: mine.shape[0]]
    rows = backs_far[0].shape[0]
    for i, back_far in enumerate(backs_far):
        back_far[...] = total[mine.shape[0] + i * rows : mine.shape[0] + (i + 1) * rows]


def backward(mine, far, pre, weights, cuts=1):
    piece = (mine.shape[0] // cuts, mine.shape[1])
    dpre0, dpre1, *backs = call(
        backward_kernel,
        [(pre[0].shape, jnp.bfloat16)] * 2
        + [(mine.shape, jnp.bfloat16)]
        + [(piece, jnp.bfloat16)] * cuts,
        mine,
        far,
        *pre,
        *weights,
    )
    return (dpre0, dpre1), *backs


def add_kernel(first, mine, far, *outs):
    mine = mine[first : first + far.shape[0]]
    total = (mine.astype(jnp.float32) + far[...].astype(jnp.float32)).astype(jnp.bfloat16)
    rows = outs[0].shape[0]
    for i, out in enumerate(outs):
        out[...] = total[i * rows : (i + 1) * rows]


def added(mine, far, group, first=0):
    kernel = functools.partial(add_kernel, first * far.shape[0])
    shape = (far.shape[0] // len(group), mine.shape[1])
    return dict(zip(group, call(kernel, [(shape, jnp.bfloat16)] * len(group), mine, far)))


def weight_kernel(lefts, rights, *refs):
    left = jnp.concatenate([ref[...] for ref in refs[:lefts]], axis=0)
    right = jnp.concatenate([ref[...] for ref in refs[lefts : lefts + rights]], axis=0)
    total = dot(left, right, ((0,), (0,)))
    outs = refs[lefts + rights :]
    rows = outs[0].shape[0]
    for i, out in enumerate(outs):
        out[...] = total[i * rows : (i + 1) * rows].astype(out.dtype)


def weight_grad(dtype, cuts, left, right):
    shape = (left[0].shape[1] // cuts, right[0].shape[1])
    kernel = functools.partial(weight_kernel, len(left), len(right))
    return call(kernel, [(shape, dtype)] * cuts, *left, *right)


def joined_kernel(own, *refs):
    out = refs[-1]
    rows = refs[0].shape[0]
    for i, ref in enumerate(refs[:-1]):
        part = slice(i * rows, (i + 1) * rows)
        out[part] = own[part] + ref[...].astype(jnp.float32)


def joined_weights(own, pieces):
    return call(joined_kernel, [(own.shape, jnp.float32)], own, *pieces)[0]


def hop(value, line):
    return swap(value, 2 * SPLIT * line, SPLIT)


def on_device(tokens, routes, gates, w_up, w_down, cotangent):
    devices = lax.axis_size("expert")
    experts_all = devices // SPLIT
    tok_local = tokens.shape[0]
    capacity = SPLIT * (
        (6 * HEADS * tok_local + 2 * experts_all * SPLIT - 1) // (2 * experts_all * SPLIT)
    )
    capacity = 16 * ((capacity + 15) // 16)
    index = lax.axis_index("expert").astype(jnp.int32).reshape(1)
    lines = experts_all // 2
    cuts = [0, lines // 2, lines - lines // 4, lines]
    near, mid, far = (list(range(a, b)) for a, b in zip(cuts, cuts[1:]))

    def joined(blocks, group):
        return blocks[group[0]] if len(group) == 1 else jnp.concatenate([blocks[m] for m in group])

    order = Order()

    def hops(blocks, group):
        return {m: order.begin(hop, blocks[m], m) for m in group}

    def come(sent):
        return dict(zip(sent, jax.tree.leaves(order.wait(*sent.values()))))

    def across(value):
        return order.begin(swap, value, 2)

    def core(value):
        return order.begin(swap, value, 1)

    def halves(blocks):
        return jnp.concatenate([blocks[m][capacity:] for m in sorted(blocks)])

    def ordered(blocks):
        return [blocks[m] for m in sorted(blocks)]

    sizes = (tok_local, experts_all, capacity)
    up_own, down_own = w_up[0], w_down[0]
    routes, gates = routes.T, gates.T

    tokens_other, routes_other = order.wait(core(tokens), core(routes))
    routes_both = (routes, routes_other)
    x_blocks = place(index, routes_both, (), (tokens, tokens_other), experts_all, capacity)
    order.done(x_blocks[0])
    x_near, x_mid, x_far = hops(x_blocks, near), hops(x_blocks, mid), hops(x_blocks, far)
    up_other, down_other = core(up_own), core(down_own)
    x0 = joined(come(x_near), near)
    x0_far = across(x0)
    *x1, up_other, down_other = order.wait(*ordered(x_mid), up_other, down_other)
    weights = (up_own, up_other, down_own, down_other)
    x1 = joined(dict(zip(mid, x1)), mid)
    x1_far = across(x1)
    cotangent_other, gates_other = order.wait(core(cotangent), core(gates))
    g_blocks = place(
        index,
        routes_both,
        (gates, gates_other),
        (cotangent, cotangent_other),
        experts_all,
        capacity,
        up_own,
        down_own,
    )
    order.done(g_blocks[0])
    pre0, hid0, part0, part0_far = forward(x0, order.wait(x0_far), weights)
    order.done(part0_far)
    m0_far = across(part0_far)
    x2 = joined(come(x_far), far)
    x2_far, g_far = across(x2), hops(g_blocks, far)
    pre1, hid1, part1, part1_far = forward(x1, order.wait(x1_far), weights)
    order.done(part1_far)
    m1_far, g_mid = across(part1_far), hops(g_blocks, mid)
    pre2, hid2, part2, part2_far = forward(x2, order.wait(x2_far), weights)
    order.done(part2_far)
    m2_far = across(part2_far)

    m_sum = added(part0, order.wait(m0_far), near)
    order.done(m_sum[near[0]])
    g2 = joined(come(g_far), far)
    g2_far = across(g2)
    m_sum |= added(part1, order.wait(m1_far), mid)
    order.done(m_sum[mid[0]])
    g_near, m_mid = hops(g_blocks, near), hops(m_sum, mid)
    g1 = joined(come(g_mid), mid)
    g1_far = across(g1)
    m_sum |= added(part2, order.wait(m2_far), far)
    order.done(m_sum[far[0]])
    m_far = hops(m_sum, far)
    g0 = joined(come(g_near), near)
    g0_far = across(g0)
    dpre2, back2, back2_far = backward(g2, order.wait(g2_far), pre2, weights)
    order.done(back2_far)
    b2_far = across(back2_far)
    m_home = come(m_mid)
    dpre1, back1, back1_far = backward(g1, order.wait(g1_far), pre1, weights)
    order.done(back1_far)
    b1_far = across(back1_far)

    b_sum = added(back2, order.wait(b2_far), far)
    order.done(b_sum[far[0]])
    b_far = hops(b_sum, far)
    m_home |= come(m_far)
    m_near = hops(m_sum, near)
    b_sum |= added(back1, order.wait(b1_far), mid)
    order.done(b_sum[mid[0]])
    b_mid = hops(b_sum, mid)
    dpre0, back0, back0_far = backward(g0, order.wait(g0_far), pre0, weights)
    order.done(back0_far)
    b0_far = across(back0_far)
    b_home = come(b_far)
    m_other = order.wait(core(halves(m_home)))

    x_all = (x0, x0_far, x1, x1_far, x2, x2_far)
    g_all = (g0, g0_far, g1, g1_far, g2, g2_far)
    hid_own, hid_other = zip(hid0, hid1, hid2)
    dpre_own, dpre_other = zip(dpre0, dpre1, dpre2)
    down_part = weight_grad(jnp.bfloat16, 2, (order.now(hid0[1]), *hid_other[1:]), g_all)
    up_part = weight_grad(jnp.bfloat16, 2, x_all, (order.now(dpre0[1]), *dpre_other[1:]))
    order.done(down_part[0])
    order.done(up_part[0])
    (down_own_part,) = weight_grad(jnp.float32, 1, (order.now(hid0[0]), *hid_own[1:]), g_all)
    order.done(down_own_part)
    (up_own_part,) = weight_grad(jnp.float32, 1, x_all, (order.now(dpre0[0]), *dpre_own[1:]))
    order.done(up_own_part)
    down_sent, up_sent = [core(part) for part in down_part], [core(part) for part in up_part]
    b_home |= come(b_mid)
    m_near = come(m_near)
    m_near_other = core(halves(m_near))
    b_sum |= added(back0, order.wait(b0_far), near)
    order.done(b_sum[near[0]])
    b_near = hops(b_sum, near)
    grad_down = joined_weights(down_own_part, order.wait(*down_sent))
    order.done(grad_down)
    mixed = collect(
        index,
        routes,
        (gates,),
        ordered(m_home | m_near),
        [order.wait(m_near_other), m_other],
        *sizes,
    )
    order.done(mixed)
    b_home |= come(b_near)
    b_other = core(halves(b_home))
    grad_up = joined_weights(up_own_part, order.wait(*up_sent))
    order.done(grad_up)
    b_other = order.wait(b_other)
    token_grad = collect(index, routes, (), ordered(b_home), [b_other], *sizes)
    return (mixed, token_grad, grad_up[None], grad_down[None])


def solution(mesh):
    placed = (
        P(("groups", "expert"), None),
        P(("groups", "expert"), None),
        P(("groups", "expert"), None),
        P("expert", None, None),
        P("expert", None, None),
        P(("groups", "expert"), None),
    )
    return jax.shard_map(
        on_device,
        mesh=mesh,
        in_specs=placed,
        out_specs=(
            P(("groups", "expert"), None),
            P(("groups", "expert"), None),
            P(("groups", "expert"), None, None),
            P(("groups", "expert"), None, None),
        ),
        check_vma=False,
    )
```
